32 devices in a mesh: pulse: 32 (over z, y, x, core), chan: 1.
Axes of the slice: x: 2, y: 2, z: 4, core: 2. Of those that a mesh axis runs over, the one named last changes fastest.
Arguments:
- echoes: bfloat16 [4, 128, 2, 5120], P('chan', 'pulse'), may hold values from -6 to 6
- replica: bfloat16 [2, 4096], replicated, may hold values from -0.0625 to 0.0625
- recon_filters: bfloat16 [4, 4, 2, 64], replicated, may hold values from -0.25 to 0.25
- span_offset: int32 [256], P('pulse'), may hold values from 0 to 4
- span_width: int32 [256], P('pulse'), may hold values from 1 to 4
- aperture_edges: int32 [2, 256], P(None, 'pulse'), may hold values from 0 to 16
Outputs:
- image: bfloat16 [4, 2, 256, 128], P(None, None, 'pulse', 'chan')
The draws below stay inside these ranges and needn't reach their ends.
All inputs are finite; a program needn't handle non-finite values.
Results may differ from the reference program's by a relative error of at most 0.012.
Values may be sent and summed in bfloat16 or wider, within the bound.
A program may use at most 64 MiB of HBM per device.

```python
import jax
import jax.numpy as jnp
from jax import lax

TAPS = 4096
AZ_TAPS = 64
MIG = 4
WMAX = 4
CHANNELS = 4
PULSES = 128
NR = 256
SAMPLES = 5120
EDGE = 16


def plant(values, stream_key, low, largest):
    longest = values.shape.index(max(values.shape))
    spots = []
    for shift in (0, 1):
        where = [jax.random.randint(jax.random.fold_in(stream_key, axis), (), 0, length) for axis, length in enumerate(values.shape)]
        where[longest] = (where[longest] + shift) % values.shape[longest]
        spots.append(tuple(where))
    return values.at[spots[0]].set(low).at[spots[1]].set(largest)


def shard_levels(key, shape, pieces, low, high):
    level = 1.0
    for position, blocks in pieces:
        heights = jax.random.uniform(jax.random.fold_in(jax.random.fold_in(key, 6), position), (blocks,), jnp.float32, low / len(pieces), high / len(pieces))
        level = level * jnp.repeat(jnp.exp(heights), shape[position] // blocks).reshape((-1,) + (1,) * (len(shape) - 1 - position))
    return level


def noise(stream_key, dims, width, most, split=(), held_as=jnp.bfloat16):
    drawn = width * jax.random.normal(stream_key, dims, jnp.float32)
    if split:
        drawn = drawn * shard_levels(stream_key, dims, split, -0.22, 0.18)
    return jnp.clip(drawn, -most, most).astype(held_as)


def setup_inputs(seed: int = 0) -> dict:
    seeds = jax.random.split(jax.random.key(seed), 7)
    echoes = noise(seeds[0], (CHANNELS, PULSES, 2, SAMPLES), 1.0, 6.0, ((1, 32),))
    replica = noise(seeds[1], (2, TAPS), (2 * TAPS) ** -0.5, 0.0625)
    recon_filters = noise(seeds[2], (CHANNELS, CHANNELS, 2, AZ_TAPS), (2 * CHANNELS * AZ_TAPS) ** -0.5, 0.25)
    span_offset = plant(jax.random.randint(seeds[3], (NR,), 0, MIG + 1), jax.random.fold_in(seeds[3], 1), 0, MIG).astype(jnp.int32)
    span_width = plant(jax.random.randint(seeds[4], (NR,), 1, WMAX + 1), jax.random.fold_in(seeds[4], 1), 1, WMAX).astype(jnp.int32)
    aperture_edges = plant(jax.random.randint(seeds[5], (2, NR), 0, EDGE + 1), jax.random.fold_in(seeds[5], 1), 0, EDGE).astype(jnp.int32)
    return {"echoes": echoes, "replica": replica, "recon_filters": recon_filters, "span_offset": span_offset, "span_width": span_width, "aperture_edges": aperture_edges}


def to_complex(part_real, part_imag):
    return part_real.astype(jnp.float32) + 1j * part_imag.astype(jnp.float32)


def reference(echoes, replica, recon_filters, span_offset, span_width, aperture_edges):
    fft_len = SAMPLES + TAPS
    kernel_spec = jnp.fft.fft(to_complex(replica[0], replica[1])[::-1], fft_len)

    def range_line(channel):
        signal = to_complex(channel[:, 0], channel[:, 1])
        full = jnp.fft.ifft(jnp.fft.fft(signal, fft_len, axis=-1) * kernel_spec[None, :], axis=-1)
        picked = full[:, TAPS - 1:TAPS - 1 + 4 * NR:4]
        return jnp.stack([jnp.real(picked).astype(jnp.bfloat16), jnp.imag(picked).astype(jnp.bfloat16)], 0)

    compressed = lax.map(range_line, echoes)
    rim_len = MIG + WMAX - 1
    padded = jnp.pad(compressed.astype(jnp.float32), ((0, 0), (0, 0), (0, 0), (0, rim_len)))
    bin_ids = jnp.arange(NR, dtype=jnp.int32)
    span_first = (bin_ids + span_offset).astype(jnp.int32)
    scale = 1.0 / span_width.astype(jnp.float32)
    migrated = jnp.zeros((CHANNELS, 2, PULSES, NR), jnp.float32)
    for shift_step in range(WMAX):
        taken = jnp.take(padded, span_first + shift_step, axis=3)
        factor = jnp.where(shift_step < span_width, scale, 0.0)
        migrated = migrated + taken * factor
    pulse_ids = jnp.arange(PULSES, dtype=jnp.int32)[:, None]
    keep_mask = ((pulse_ids >= aperture_edges[0][None, :]) & (pulse_ids < PULSES - aperture_edges[1][None, :])).astype(jnp.float32)
    corrected = (migrated * keep_mask).astype(jnp.bfloat16)
    field = to_complex(corrected[:, 0], corrected[:, 1]).transpose(0, 2, 1)
    half_taps = AZ_TAPS // 2
    field = jnp.pad(field, ((0, 0), (0, 0), (half_taps, half_taps)))
    az_len = PULSES + 2 * AZ_TAPS
    field_spec = jnp.fft.fft(field, az_len, axis=-1)
    filter_spec = jnp.fft.fft(to_complex(recon_filters[:, :, 0], recon_filters[:, :, 1])[..., ::-1], az_len, axis=-1)
    image_spec = jnp.einsum('crl,scl->srl', field_spec, filter_spec, precision=lax.Precision.HIGHEST)
    image = jnp.fft.ifft(image_spec, axis=-1)[:, :, AZ_TAPS - 1:AZ_TAPS - 1 + PULSES]
    return jnp.stack([jnp.real(image), jnp.imag(image)], 1).astype(jnp.bfloat16)
```

```python
import functools

import jax
import jax.numpy as jnp
from jax import lax
from jax.experimental import pallas as pl
from jax.experimental.pallas import tpu as pltpu
from jax.sharding import PartitionSpec as P

LANES = 128
STEP = 4
BLOCK = LANES // STEP
NT = (((1,), (1,)), ((), ()))


def dot_nt(a, b):
    return lax.dot_general(a, b, NT, preferred_element_type=jnp.float32)


def range_rows(replica_ref, bmat_ref, bins, depth):
    span = 2 * bins
    windows = BLOCK // bins
    rows = BLOCK + bins
    taps = replica_ref.shape[1]
    replica = replica_ref[...].astype(jnp.float32)
    shifted = []
    for part in range(2):
        row = jnp.concatenate([replica[part : part + 1], jnp.zeros((1, depth - taps), jnp.float32)], axis=1)
        shifted.append(
            pltpu.roll(jnp.broadcast_to(row, (rows, depth)), 0, 1, stride=STEP, stride_axis=0)
        )
    real, imag = shifted
    half = windows * 2 * span
    for window in range(windows):
        low = window * bins
        real_part = real[low : low + span].astype(jnp.bfloat16)
        imag_part = imag[low : low + span].astype(jnp.bfloat16)
        at = window * 2 * span
        bmat_ref[at : at + span, :] = real_part
        bmat_ref[at + span : at + 2 * span, :] = imag_part
        bmat_ref[half + at : half + at + span, :] = -imag_part
        bmat_ref[half + at + span : half + at + 2 * span, :] = real_part


def azimuth_rows(filters_ref, tt_ref, step):
    samples, channels, _, taps = filters_ref.shape
    for s in range(samples):
        for c in range(channels):
            taps_row = filters_ref[s, c].astype(jnp.float32)
            taps_row = jnp.concatenate([taps_row, jnp.zeros((2, LANES - taps), jnp.float32)], axis=1)
            real, imag = [
                pltpu.roll(
                    jnp.broadcast_to(taps_row[part : part + 1], (step, LANES)), 0, 1, stride=1, stride_axis=0
                ).astype(jnp.bfloat16)
                for part in range(2)
            ]
            top, left = s * 2 * step, c * 2 * LANES
            tt_ref[top : top + step, left : left + LANES] = real
            tt_ref[top + step : top + 2 * step, left : left + LANES] = imag
            tt_ref[top : top + step, left + LANES : left + 2 * LANES] = -imag
            tt_ref[top + step : top + 2 * step, left + LANES : left + 2 * LANES] = real


def column(values, count):
    ids = lax.broadcasted_iota(jnp.int32, (count, LANES), 0)
    total = jnp.zeros((count, LANES), jnp.int32)
    for r in range(count):
        total = jnp.where(ids == r, values(r), total)
    return total


def kernel(
    n, whole_image,
    echoes_ref, replica_ref, filters_ref, offset_ref, width_ref, edges_ref,
    out_ref,
    raw, lines, bmat, tt, product, send, recv, turned,
    in_sem, send_sem, recv_sem,
):
    me = lax.axis_index("pulse")
    channels, pulses, _, samples = echoes_ref.shape
    taps = replica_ref.shape[1]
    depth = bmat.shape[1]
    bin_count = (samples - taps) // STEP
    bins = bin_count // n
    span = 2 * bins
    windows = BLOCK // bins
    piece = 2 * span
    pairs = channels * pulses

    fetch = pltpu.make_async_copy(echoes_ref, raw, in_sem)
    fetch.start()

    barrier = pltpu.get_barrier_semaphore()

    @pl.loop(1, n)
    def _(k):
        pl.semaphore_signal(
            barrier, inc=1, device_id={"pulse": lax.rem(me + k, n)}, device_id_type=pl.DeviceIdType.MESH
        )

    range_rows(replica_ref, bmat, bins, depth)
    fetch.wait()
    for c in range(channels):
        for p in range(pulses):
            at = 2 * (c * pulses + p)
            lines[at : at + 2, :samples] = raw[c, p]
    lines[:, samples:] = jnp.zeros((2 * pairs, lines.shape[1] - samples), lines.dtype)

    blocks = bin_count // BLOCK
    group = min(blocks, 8)
    rows = 2 * pulses
    lane = lax.broadcasted_iota(jnp.int32, (group * pulses, LANES), 1)
    for first in range(0, blocks, group):
        rows_in = jnp.concatenate(
            [lines[:, LANES * a : LANES * a + depth] for a in range(first, first + group)], axis=0
        )
        result = dot_nt(rows_in, bmat[...])
        for a in range(group):
            for c in range(channels):
                at = (a * channels + c) * rows
                for half in range(2):
                    product[half, c, a * rows : (a + 1) * rows, :] = result[
                        at : at + rows, half * LANES : (half + 1) * LANES
                    ]
        by_channel = [
            product[0, c, pl.ds(0, group * pulses, stride=2), :]
            + product[1, c, pl.ds(1, group * pulses, stride=2), :]
            for c in range(channels)
        ]
        for w in range(windows):
            message = None
            for c in range(channels):
                shift = (piece * (c - w)) % LANES
                moved = pltpu.roll(by_channel[c], shift, 1) if shift else by_channel[c]
                message = moved if c == 0 else jnp.where(lane >= piece * c, moved, message)
            for a in range(group):
                send[(first + a) * windows + w] = message[a * pulses : (a + 1) * pulses].astype(send.dtype)

    pl.semaphore_wait(barrier, n - 1)

    @pl.loop(1, n)
    def _(k):
        to = lax.rem(me + k, n)
        pltpu.make_async_remote_copy(
            src_ref=send.at[to], dst_ref=recv.at[me], send_sem=send_sem, recv_sem=recv_sem,
            device_id={"pulse": to}, device_id_type=pl.DeviceIdType.MESH,
        ).start()

    recv[me] = send[me]

    all_pulses = n * pulses
    row_id = lax.broadcasted_iota(jnp.int32, (bins, LANES), 0)
    lane_id = lax.broadcasted_iota(jnp.int32, (bins, LANES), 1)
    first_bin = row_id + column(lambda r: offset_ref[r], bins)
    width = column(lambda r: width_ref[r], bins)
    low_edge = column(lambda r: edges_ref[0, r], bins)
    high_edge = all_pulses - column(lambda r: edges_ref[1, r], bins)
    place = lane_id % span
    chosen = (place >= first_bin) & (place < first_bin + width) & (place + me * bins < bin_count)
    select = jnp.concatenate(
        [
            jnp.where(chosen & (lane_id // span == g), 1.0, 0.0)
            for g in range(2 * channels)
        ],
        axis=0,
    ).astype(jnp.bfloat16)
    scale = 1.0 / width.astype(jnp.float32)

    margin = (turned.shape[0] - all_pulses) // 2
    if whole_image:
        turned[0:margin, :] = jnp.zeros((margin, LANES), jnp.float32)
        turned[margin + all_pulses :, :] = jnp.zeros((margin, LANES), jnp.float32)
        azimuth_rows(filters_ref, tt, tt.shape[0] // (2 * filters_ref.shape[0]))

    pltpu.make_async_copy(send.at[pl.ds(0, n - 1)], recv.at[pl.ds(0, n - 1)], recv_sem).wait()

    for i in range(n):
        turned[margin + i * pulses : margin + (i + 1) * pulses, :] = recv[i].astype(jnp.float32)

    def corrected(start):
        taken = dot_nt(select, turned[start : start + LANES, :].astype(jnp.bfloat16))
        pulse = lane_id + (start - margin)
        weight = jnp.where((pulse >= low_edge) & (pulse < high_edge), scale, 0.0)
        return [taken[g * bins : (g + 1) * bins] * weight for g in range(2 * channels)]

    if whole_image:
        samples_out = filters_ref.shape[0]
        step = LANES // 2
        rows_in = jnp.concatenate(
            [jnp.concatenate(corrected(start), axis=1) for start in range(0, all_pulses, step)], axis=0
        ).astype(jnp.bfloat16)
        image = dot_nt(rows_in, tt[...])
        left = lane_id < step
        for s in range(samples_out):
            for b in range(all_pulses // LANES):
                at = 2 * b * bins
                early = image[at : at + bins, s * LANES : (s + 1) * LANES]
                late = image[at + bins : at + 2 * bins, s * LANES : (s + 1) * LANES]
                real = jnp.where(left, early, pltpu.roll(late, step, 1))
                imag = jnp.where(left, pltpu.roll(early, step, 1), late)
                out_ref[s, 0, :, b * LANES : (b + 1) * LANES] = real.astype(out_ref.dtype)
                out_ref[s, 1, :, b * LANES : (b + 1) * LANES] = imag.astype(out_ref.dtype)
    else:
        for b in range(all_pulses // LANES):
            for g, part in enumerate(corrected(b * LANES)):
                out_ref[g // 2, g % 2, :, b * LANES : (b + 1) * LANES] = part.astype(out_ref.dtype)

    pltpu.make_async_copy(send.at[pl.ds(0, n - 1)], recv.at[pl.ds(0, n - 1)], send_sem).wait()


def run_kernel(echoes, replica, recon_filters, span_offset, span_width, aperture_edges, whole_image):
    n = lax.axis_size("pulse")
    channels, pulses, _, samples = echoes.shape
    taps = replica.shape[1]
    bin_count = (samples - taps) // STEP
    bins = bin_count // n
    span = 2 * bins
    all_pulses = n * pulses
    blocks = bin_count // BLOCK
    group = min(blocks, 8)
    assert BLOCK % bins == 0 and channels * 2 * span == LANES and channels == BLOCK // bins
    assert blocks % group == 0 and all_pulses % LANES == 0
    depth = taps + 2 * LANES
    samples_out, _, _, az_taps = recon_filters.shape
    step = LANES // 2
    assert az_taps == step
    if whole_image:
        margin = az_taps // 2
        out_shape = (samples_out, 2, bins, all_pulses)
        tt_shape = (samples_out * 2 * step, channels * 2 * LANES)
    else:
        margin = 0
        out_shape = (channels, 2, bins, all_pulses)
        tt_shape = (16, LANES)
    vmem = pl.BlockSpec(memory_space=pltpu.VMEM)
    smem = pl.BlockSpec(memory_space=pltpu.SMEM)
    return pl.pallas_call(
        functools.partial(kernel, n, whole_image),
        out_shape=jax.ShapeDtypeStruct(out_shape, jnp.bfloat16),
        in_specs=[pl.BlockSpec(memory_space=pl.ANY), vmem, vmem, smem, smem, smem],
        out_specs=vmem,
        scratch_shapes=[
            pltpu.VMEM(echoes.shape, jnp.bfloat16),
            pltpu.VMEM((2 * channels * pulses, samples + LANES), jnp.bfloat16),
            pltpu.VMEM((2 * LANES, depth), jnp.bfloat16),
            pltpu.VMEM(tt_shape, jnp.bfloat16),
            pltpu.VMEM((2, channels, group * 2 * pulses, LANES), jnp.float32),
            pltpu.VMEM((n, pulses, LANES), jnp.bfloat16),
            pltpu.VMEM((n, pulses, LANES), jnp.bfloat16),
            pltpu.VMEM((all_pulses + 2 * margin, LANES), jnp.float32),
            pltpu.SemaphoreType.DMA,
            pltpu.SemaphoreType.DMA,
            pltpu.SemaphoreType.DMA,
        ],
        compiler_params=pltpu.CompilerParams(
            collective_id=0, has_side_effects=True, vmem_limit_bytes=48 * 1024 * 1024
        ),
    )(echoes, replica, recon_filters, span_offset, span_width, aperture_edges)


def with_neighbours(cells, axis, dim, width):
    count = lax.axis_size(axis)
    head = lax.slice_in_dim(cells, 0, width, axis=dim)
    tail = lax.slice_in_dim(cells, cells.shape[dim] - width, cells.shape[dim], axis=dim)
    up = [(i, i + 1) for i in range(count - 1)]
    down = [(i + 1, i) for i in range(count - 1)]
    return jnp.concatenate(
        [lax.ppermute(tail, axis, up), cells, lax.ppermute(head, axis, down)], axis=dim
    )


def azimuth(padded, filters):
    channels, _, bin_count, padded_len = padded.shape
    subbands = filters.shape[0]
    tap_count = filters.shape[3]
    pulses = padded_len - tap_count
    span_len = tap_count + 4
    step_count = span_len // 4
    quartets = padded.reshape(channels, 2, bin_count, padded_len // 4, 4)
    window = jnp.stack(
        [quartets[:, :, :, first : first + pulses // 4, :] for first in range(step_count)], 4
    )
    window = window.transpose(2, 3, 0, 1, 4, 5).reshape(
        bin_count * (pulses // 4), channels * 2 * span_len
    )
    offset = jnp.arange(span_len)[:, None] - jnp.arange(4)[None, :]
    inside = (offset >= 0) & (offset < tap_count)
    picked = jnp.where(inside, jnp.take(filters, jnp.clip(offset, 0, tap_count - 1), axis=3), 0)
    real, imag = picked[:, :, 0], picked[:, :, 1]
    matrix = jnp.stack([jnp.stack([real, imag], 3), jnp.stack([-imag, real], 3)], 2)
    matrix = matrix.transpose(1, 2, 3, 0, 4, 5).reshape(channels * 2 * span_len, subbands * 8)
    result = jnp.dot(window, matrix, preferred_element_type=jnp.float32)
    result = result.reshape(bin_count, pulses // 4, subbands, 2, 4).transpose(2, 3, 0, 1, 4)
    return result.reshape(subbands, 2, bin_count, pulses)


def body(echoes, replica, recon_filters, span_offset, span_width, aperture_edges):
    operands = (echoes, replica, recon_filters, span_offset, span_width, aperture_edges)
    if lax.axis_size("chan") == 1 and echoes.shape[0] == recon_filters.shape[1]:
        return run_kernel(*operands, whole_image=True)
    corrected = run_kernel(*operands, whole_image=False)
    corrected = lax.all_to_all(corrected, "chan", split_axis=3, concat_axis=0, tiled=True)
    padded = with_neighbours(corrected, "chan", 3, recon_filters.shape[3] // 2)
    return azimuth(padded, recon_filters).astype(jnp.bfloat16)


def solution(mesh):
    return jax.shard_map(
        body,
        mesh=mesh,
        in_specs=(
            P("chan", "pulse", None, None),
            P(),
            P(),
            P("pulse"),
            P("pulse"),
            P(None, "pulse"),
        ),
        out_specs=P(None, None, "pulse", "chan"),
        check_vma=False,
    )
```

```python
import functools

import jax
import jax.numpy as jnp
from jax import lax
from jax.experimental import pallas as pl
from jax.experimental.pallas import tpu as pltpu
from jax.sharding import PartitionSpec as P

LANES = 128
STEP = 4
BLOCK = LANES // STEP
NT = (((1,), (1,)), ((), ()))


def dot_nt(a, b):
    return lax.dot_general(a, b, NT, preferred_element_type=jnp.float32)


def range_rows(replica_ref, bmat_ref, bins, depth):
    span = 2 * bins
    windows = BLOCK // bins
    rows = BLOCK + bins
    taps = replica_ref.shape[1]
    replica = replica_ref[...].astype(jnp.float32)
    shifted = []
    for part in range(2):
        row = jnp.concatenate([replica[part : part + 1], jnp.zeros((1, depth - taps), jnp.float32)], axis=1)
        shifted.append(
            pltpu.roll(jnp.broadcast_to(row, (rows, depth)), 0, 1, stride=STEP, stride_axis=0)
        )
    real, imag = shifted
    half = windows * 2 * span
    for window in range(windows):
        low = window * bins
        real_part = real[low : low + span].astype(jnp.bfloat16)
        imag_part = imag[low : low + span].astype(jnp.bfloat16)
        at = window * 2 * span
        bmat_ref[at : at + span, :] = real_part
        bmat_ref[at + span : at + 2 * span, :] = imag_part
        bmat_ref[half + at : half + at + span, :] = -imag_part
        bmat_ref[half + at + span : half + at + 2 * span, :] = real_part


def azimuth_rows(filters_ref, tt_ref, step):
    samples, channels, _, taps = filters_ref.shape
    for s in range(samples):
        for c in range(channels):
            taps_row = filters_ref[s, c].astype(jnp.float32)
            taps_row = jnp.concatenate([taps_row, jnp.zeros((2, LANES - taps), jnp.float32)], axis=1)
            real, imag = [
                pltpu.roll(
                    jnp.broadcast_to(taps_row[part : part + 1], (step, LANES)), 0, 1, stride=1, stride_axis=0
                ).astype(jnp.bfloat16)
                for part in range(2)
            ]
            top, left = s * 2 * step, c * 2 * LANES
            tt_ref[top : top + step, left : left + LANES] = real
            tt_ref[top + step : top + 2 * step, left : left + LANES] = imag
            tt_ref[top : top + step, left + LANES : left + 2 * LANES] = -imag
            tt_ref[top + step : top + 2 * step, left + LANES : left + 2 * LANES] = real


def column(values, count):
    ids = lax.broadcasted_iota(jnp.int32, (count, LANES), 0)
    total = jnp.zeros((count, LANES), jnp.int32)
    for r in range(count):
        total = jnp.where(ids == r, values(r), total)
    return total


def kernel(
    n, whole_image,
    echoes_in, replica_in, filters_in, offset_in, width_in, edges_in,
    out_ref,
    raw, replica_ref, filters_ref, offset_ref, width_ref, edges_ref,
    lines, bmat, tt, product, send, recv, turned,
    in_sem, send_sem, recv_sem,
):
    me = lax.axis_index("pulse")
    channels, pulses, _, samples = raw.shape
    taps = replica_ref.shape[1]
    depth = bmat.shape[1]
    bin_count = (samples - taps) // STEP
    bins = bin_count // n
    span = 2 * bins
    windows = BLOCK // bins
    piece = 2 * span
    pairs = channels * pulses

    replica_fetch, echoes_fetch, *small_fetches = [
        pltpu.make_async_copy(source, held, in_sem.at[i])
        for i, (source, held) in enumerate(
            [
                (replica_in, replica_ref),
                (echoes_in, raw),
                (filters_in, filters_ref),
                (offset_in, offset_ref),
                (width_in, width_ref),
                (edges_in, edges_ref),
            ]
        )
    ]
    for fetch in [replica_fetch, echoes_fetch, *small_fetches]:
        fetch.start()

    barrier = pltpu.get_barrier_semaphore()

    @pl.loop(1, n)
    def _(k):
        pl.semaphore_signal(
            barrier, inc=1, device_id={"pulse": jnp.where(me + k < n, me + k, me + k - n)}, device_id_type=pl.DeviceIdType.MESH
        )

    replica_fetch.wait()
    range_rows(replica_ref, bmat, bins, depth)
    echoes_fetch.wait()
    for c in range(channels):
        for p in range(pulses):
            at = 2 * (c * pulses + p)
            lines[at : at + 2, :samples] = raw[c, p]
    lines[:, samples:] = jnp.zeros((2 * pairs, lines.shape[1] - samples), lines.dtype)

    blocks = bin_count // BLOCK
    group = min(blocks, 8)
    rows = 2 * pulses
    lane = lax.broadcasted_iota(jnp.int32, (group * pulses, LANES), 1)
    for first in range(0, blocks, group):
        rows_in = jnp.concatenate(
            [lines[:, LANES * a : LANES * a + depth] for a in range(first, first + group)], axis=0
        )
        result = dot_nt(rows_in, bmat[...])
        for a in range(group):
            for c in range(channels):
                at = (a * channels + c) * rows
                for half in range(2):
                    product[half, c, a * rows : (a + 1) * rows, :] = result[
                        at : at + rows, half * LANES : (half + 1) * LANES
                    ]
        by_channel = [
            product[0, c, pl.ds(0, group * pulses, stride=2), :]
            + product[1, c, pl.ds(1, group * pulses, stride=2), :]
            for c in range(channels)
        ]
        for w in range(windows):
            message = None
            for c in range(channels):
                shift = (piece * (c - w)) % LANES
                moved = pltpu.roll(by_channel[c], shift, 1) if shift else by_channel[c]
                message = moved if c == 0 else jnp.where(lane >= piece * c, moved, message)
            for a in range(group):
                send[(first + a) * windows + w] = message[a * pulses : (a + 1) * pulses].astype(send.dtype)

    pl.semaphore_wait(barrier, n - 1)

    @pl.loop(1, n)
    def _(k):
        to = jnp.where(me + k < n, me + k, me + k - n)
        pltpu.make_async_remote_copy(
            src_ref=send.at[to], dst_ref=recv.at[me], send_sem=send_sem, recv_sem=recv_sem,
            device_id={"pulse": to}, device_id_type=pl.DeviceIdType.MESH,
        ).start()

    recv[me] = send[me]

    for fetch in small_fetches:
        fetch.wait()
    all_pulses = n * pulses
    row_id = lax.broadcasted_iota(jnp.int32, (bins, LANES), 0)
    lane_id = lax.broadcasted_iota(jnp.int32, (bins, LANES), 1)
    first_bin = row_id + column(lambda r: offset_ref[r], bins)
    width = column(lambda r: width_ref[r], bins)
    low_edge = column(lambda r: edges_ref[0, r], bins)
    high_edge = all_pulses - column(lambda r: edges_ref[1, r], bins)
    place = lane_id % span
    chosen = (place >= first_bin) & (place < first_bin + width) & (place + me * bins < bin_count)
    select = jnp.concatenate(
        [
            jnp.where(chosen & (lane_id // span == g), 1.0, 0.0)
            for g in range(2 * channels)
        ],
        axis=0,
    ).astype(jnp.bfloat16)
    scale = 1.0 / width.astype(jnp.float32)

    margin = (turned.shape[0] - all_pulses) // 2
    if whole_image:
        turned[0:margin, :] = jnp.zeros((margin, LANES), jnp.float32)
        turned[margin + all_pulses :, :] = jnp.zeros((margin, LANES), jnp.float32)
        azimuth_rows(filters_ref, tt, tt.shape[0] // (2 * filters_ref.shape[0]))

    pltpu.make_async_copy(send.at[pl.ds(0, n - 1)], recv.at[pl.ds(0, n - 1)], recv_sem).wait()

    for i in range(n):
        turned[margin + i * pulses : margin + (i + 1) * pulses, :] = recv[i].astype(jnp.float32)

    def corrected(start):
        taken = dot_nt(select, turned[start : start + LANES, :].astype(jnp.bfloat16))
        pulse = lane_id + (start - margin)
        weight = jnp.where((pulse >= low_edge) & (pulse < high_edge), scale, 0.0)
        return [taken[g * bins : (g + 1) * bins] * weight for g in range(2 * channels)]

    if whole_image:
        samples_out = filters_ref.shape[0]
        step = LANES // 2
        rows_in = jnp.concatenate(
            [jnp.concatenate(corrected(start), axis=1) for start in range(0, all_pulses, step)], axis=0
        ).astype(jnp.bfloat16)
        image = dot_nt(rows_in, tt[...])
        left = lane_id < step
        for s in range(samples_out):
            for b in range(all_pulses // LANES):
                at = 2 * b * bins
                early = image[at : at + bins, s * LANES : (s + 1) * LANES]
                late = image[at + bins : at + 2 * bins, s * LANES : (s + 1) * LANES]
                real = jnp.where(left, early, pltpu.roll(late, step, 1))
                imag = jnp.where(left, pltpu.roll(early, step, 1), late)
                out_ref[s, 0, :, b * LANES : (b + 1) * LANES] = real.astype(out_ref.dtype)
                out_ref[s, 1, :, b * LANES : (b + 1) * LANES] = imag.astype(out_ref.dtype)
    else:
        for b in range(all_pulses // LANES):
            for g, part in enumerate(corrected(b * LANES)):
                out_ref[g // 2, g % 2, :, b * LANES : (b + 1) * LANES] = part.astype(out_ref.dtype)

    pltpu.make_async_copy(send.at[pl.ds(0, n - 1)], recv.at[pl.ds(0, n - 1)], send_sem).wait()


def run_kernel(echoes, replica, recon_filters, span_offset, span_width, aperture_edges, whole_image):
    n = lax.axis_size("pulse")
    channels, pulses, _, samples = echoes.shape
    taps = replica.shape[1]
    bin_count = (samples - taps) // STEP
    bins = bin_count // n
    span = 2 * bins
    all_pulses = n * pulses
    blocks = bin_count // BLOCK
    group = min(blocks, 8)
    assert BLOCK % bins == 0 and channels * 2 * span == LANES and channels == BLOCK // bins
    assert blocks % group == 0 and all_pulses % LANES == 0
    depth = taps + 2 * LANES
    samples_out, _, _, az_taps = recon_filters.shape
    step = LANES // 2
    assert az_taps == step
    if whole_image:
        margin = az_taps // 2
        out_shape = (samples_out, 2, bins, all_pulses)
        tt_shape = (samples_out * 2 * step, channels * 2 * LANES)
    else:
        margin = 0
        out_shape = (channels, 2, bins, all_pulses)
        tt_shape = (16, LANES)
    vmem = pl.BlockSpec(memory_space=pltpu.VMEM)
    return pl.pallas_call(
        functools.partial(kernel, n, whole_image),
        out_shape=jax.ShapeDtypeStruct(out_shape, jnp.bfloat16),
        in_specs=[pl.BlockSpec(memory_space=pl.ANY)] * 6,
        out_specs=vmem,
        scratch_shapes=[
            pltpu.VMEM(echoes.shape, jnp.bfloat16),
            pltpu.VMEM(replica.shape, jnp.bfloat16),
            pltpu.VMEM(recon_filters.shape, jnp.bfloat16),
            pltpu.SMEM(span_offset.shape, jnp.int32),
            pltpu.SMEM(span_width.shape, jnp.int32),
            pltpu.SMEM(aperture_edges.shape, jnp.int32),
            pltpu.VMEM((2 * channels * pulses, samples + LANES), jnp.bfloat16),
            pltpu.VMEM((2 * LANES, depth), jnp.bfloat16),
            pltpu.VMEM(tt_shape, jnp.bfloat16),
            pltpu.VMEM((2, channels, group * 2 * pulses, LANES), jnp.float32),
            pltpu.VMEM((n, pulses, LANES), jnp.bfloat16),
            pltpu.VMEM((n, pulses, LANES), jnp.bfloat16),
            pltpu.VMEM((all_pulses + 2 * margin, LANES), jnp.float32),
            pltpu.SemaphoreType.DMA((6,)),
            pltpu.SemaphoreType.DMA,
            pltpu.SemaphoreType.DMA,
        ],
        compiler_params=pltpu.CompilerParams(
            collective_id=0, has_side_effects=True, vmem_limit_bytes=64 * 1024 * 1024 - 20 * 1024
        ),
    )(echoes, replica, recon_filters, span_offset, span_width, aperture_edges)


def with_neighbours(cells, axis, dim, width):
    count = lax.axis_size(axis)
    head = lax.slice_in_dim(cells, 0, width, axis=dim)
    tail = lax.slice_in_dim(cells, cells.shape[dim] - width, cells.shape[dim], axis=dim)
    up = [(i, i + 1) for i in range(count - 1)]
    down = [(i + 1, i) for i in range(count - 1)]
    return jnp.concatenate(
        [lax.ppermute(tail, axis, up), cells, lax.ppermute(head, axis, down)], axis=dim
    )


def azimuth(padded, filters):
    channels, _, bin_count, padded_len = padded.shape
    subbands = filters.shape[0]
    tap_count = filters.shape[3]
    pulses = padded_len - tap_count
    span_len = tap_count + 4
    step_count = span_len // 4
    quartets = padded.reshape(channels, 2, bin_count, padded_len // 4, 4)
    window = jnp.stack(
        [quartets[:, :, :, first : first + pulses // 4, :] for first in range(step_count)], 4
    )
    window = window.transpose(2, 3, 0, 1, 4, 5).reshape(
        bin_count * (pulses // 4), channels * 2 * span_len
    )
    offset = jnp.arange(span_len)[:, None] - jnp.arange(4)[None, :]
    inside = (offset >= 0) & (offset < tap_count)
    picked = jnp.where(inside, jnp.take(filters, jnp.clip(offset, 0, tap_count - 1), axis=3), 0)
    real, imag = picked[:, :, 0], picked[:, :, 1]
    matrix = jnp.stack([jnp.stack([real, imag], 3), jnp.stack([-imag, real], 3)], 2)
    matrix = matrix.transpose(1, 2, 3, 0, 4, 5).reshape(channels * 2 * span_len, subbands * 8)
    result = jnp.dot(window, matrix, preferred_element_type=jnp.float32)
    result = result.reshape(bin_count, pulses // 4, subbands, 2, 4).transpose(2, 3, 0, 1, 4)
    return result.reshape(subbands, 2, bin_count, pulses)


def body(echoes, replica, recon_filters, span_offset, span_width, aperture_edges):
    operands = (echoes, replica, recon_filters, span_offset, span_width, aperture_edges)
    if lax.axis_size("chan") == 1 and echoes.shape[0] == recon_filters.shape[1]:
        return run_kernel(*operands, whole_image=True)
    corrected = run_kernel(*operands, whole_image=False)
    corrected = lax.all_to_all(corrected, "chan", split_axis=3, concat_axis=0, tiled=True)
    padded = with_neighbours(corrected, "chan", 3, recon_filters.shape[3] // 2)
    return azimuth(padded, recon_filters).astype(jnp.bfloat16)


def solution(mesh):
    return jax.shard_map(
        body,
        mesh=mesh,
        in_specs=(
            P("chan", "pulse", None, None),
            P(),
            P(),
            P("pulse"),
            P("pulse"),
            P(None, "pulse"),
        ),
        out_specs=P(None, None, "pulse", "chan"),
        check_vma=False,
    )
```

```python
import functools

import jax
import jax.numpy as jnp
from jax import lax
from jax.experimental import pallas as pl
from jax.experimental.pallas import tpu as pltpu
from jax.sharding import PartitionSpec as P

LANES = 128
STEP = 4
BLOCK = LANES // STEP
NT = (((1,), (1,)), ((), ()))


def dot_nt(a, b):
    return lax.dot_general(a, b, NT, preferred_element_type=jnp.float32)


def range_rows(replica_ref, bmat_ref, bins, depth):
    span = 2 * bins
    windows = BLOCK // bins
    rows = BLOCK + bins
    taps = replica_ref.shape[1]
    replica = replica_ref[...].astype(jnp.float32)
    shifted = []
    for part in range(2):
        row = jnp.concatenate([replica[part : part + 1], jnp.zeros((1, depth - taps), jnp.float32)], axis=1)
        shifted.append(
            pltpu.roll(jnp.broadcast_to(row, (rows, depth)), 0, 1, stride=STEP, stride_axis=0)
        )
    real, imag = shifted
    half = windows * 2 * span
    for window in range(windows):
        low = window * bins
        real_part = real[low : low + span].astype(jnp.bfloat16)
        imag_part = imag[low : low + span].astype(jnp.bfloat16)
        at = window * 2 * span
        bmat_ref[at : at + span, :] = real_part
        bmat_ref[at + span : at + 2 * span, :] = imag_part
        bmat_ref[half + at : half + at + span, :] = -imag_part
        bmat_ref[half + at + span : half + at + 2 * span, :] = real_part


def azimuth_rows(filters_ref, tt_ref, step):
    samples, channels, _, taps = filters_ref.shape
    for s in range(samples):
        for c in range(channels):
            taps_row = filters_ref[s, c].astype(jnp.float32)
            taps_row = jnp.concatenate([taps_row, jnp.zeros((2, LANES - taps), jnp.float32)], axis=1)
            real, imag = [
                pltpu.roll(
                    jnp.broadcast_to(taps_row[part : part + 1], (step, LANES)), 0, 1, stride=1, stride_axis=0
                ).astype(jnp.bfloat16)
                for part in range(2)
            ]
            top, left = s * 2 * step, c * 2 * LANES
            tt_ref[top : top + step, left : left + LANES] = real
            tt_ref[top + step : top + 2 * step, left : left + LANES] = imag
            tt_ref[top : top + step, left + LANES : left + 2 * LANES] = -imag
            tt_ref[top + step : top + 2 * step, left + LANES : left + 2 * LANES] = real


def over_others(n):
    def run(step):
        if n <= 32:
            for k in range(1, n):
                step(k)
        else:
            pl.loop(1, n)(step)

    return run


def column(values, count):
    ids = lax.broadcasted_iota(jnp.int32, (count, LANES), 0)
    total = jnp.zeros((count, LANES), jnp.int32)
    for r in range(count):
        total = jnp.where(ids == r, values(r), total)
    return total


def kernel(
    n, whole_image,
    echoes_in, replica_in, filters_in, offset_in, width_in, edges_in,
    out_ref,
    replica_ref, filters_ref, offset_ref, width_ref, edges_ref,
    lines, bmat, tt, product, send, recv, turned,
    in_sem, send_sem, recv_sem,
):
    me = lax.axis_index("pulse")
    channels, pulses, _, samples = echoes_in.shape
    taps = replica_ref.shape[1]
    depth = bmat.shape[1]
    bin_count = (samples - taps) // STEP
    bins = bin_count // n
    span = 2 * bins
    windows = BLOCK // bins
    piece = 2 * span
    pairs = channels * pulses

    replica_fetch, echoes_fetch, *small_fetches = [
        pltpu.make_async_copy(source, held, in_sem.at[i])
        for i, (source, held) in enumerate(
            [
                (replica_in, replica_ref),
                (echoes_in.reshape(2 * channels * pulses, samples), lines.at[:, pl.ds(0, samples)]),
                (filters_in, filters_ref),
                (offset_in, offset_ref),
                (width_in, width_ref),
                (edges_in, edges_ref),
            ]
        )
    ]
    for fetch in [replica_fetch, echoes_fetch, *small_fetches]:
        fetch.start()

    barrier = pltpu.get_barrier_semaphore()

    @over_others(n)
    def _(k):
        pl.semaphore_signal(
            barrier, inc=1, device_id={"pulse": jnp.where(me + k < n, me + k, me + k - n)}, device_id_type=pl.DeviceIdType.MESH
        )

    replica_fetch.wait()
    range_rows(replica_ref, bmat, bins, depth)
    echoes_fetch.wait()
    lines[:, samples:] = jnp.zeros((2 * pairs, lines.shape[1] - samples), lines.dtype)

    blocks = bin_count // BLOCK
    group = min(blocks, 8)
    rows = 2 * pulses
    lane = lax.broadcasted_iota(jnp.int32, (group * pulses, LANES), 1)
    for first in range(0, blocks, group):
        rows_in = jnp.concatenate(
            [lines[:, LANES * a : LANES * a + depth] for a in range(first, first + group)], axis=0
        )
        result = dot_nt(rows_in, bmat[...])
        for a in range(group):
            for c in range(channels):
                at = (a * channels + c) * rows
                for half in range(2):
                    product[half, c, a * rows : (a + 1) * rows, :] = result[
                        at : at + rows, half * LANES : (half + 1) * LANES
                    ]
        by_channel = [
            product[0, c, pl.ds(0, group * pulses, stride=2), :]
            + product[1, c, pl.ds(1, group * pulses, stride=2), :]
            for c in range(channels)
        ]
        for w in range(windows):
            message = None
            for c in range(channels):
                shift = (piece * (c - w)) % LANES
                moved = pltpu.roll(by_channel[c], shift, 1) if shift else by_channel[c]
                message = moved if c == 0 else jnp.where(lane >= piece * c, moved, message)
            for a in range(group):
                send[(first + a) * windows + w] = message[a * pulses : (a + 1) * pulses].astype(send.dtype)

    pl.semaphore_wait(barrier, n - 1)

    @over_others(n)
    def _(k):
        to = jnp.where(me + k < n, me + k, me + k - n)
        pltpu.make_async_remote_copy(
            src_ref=send.at[to], dst_ref=recv.at[me], send_sem=send_sem, recv_sem=recv_sem,
            device_id={"pulse": to}, device_id_type=pl.DeviceIdType.MESH,
        ).start()

    recv[me] = send[me]

    for fetch in small_fetches:
        fetch.wait()
    all_pulses = n * pulses
    row_id = lax.broadcasted_iota(jnp.int32, (bins, LANES), 0)
    lane_id = lax.broadcasted_iota(jnp.int32, (bins, LANES), 1)
    first_bin = row_id + column(lambda r: offset_ref[r], bins)
    width = column(lambda r: width_ref[r], bins)
    low_edge = column(lambda r: edges_ref[0, r], bins)
    high_edge = all_pulses - column(lambda r: edges_ref[1, r], bins)
    place = lane_id % span
    chosen = (place >= first_bin) & (place < first_bin + width) & (place + me * bins < bin_count)
    select = jnp.concatenate(
        [
            jnp.where(chosen & (lane_id // span == g), 1.0, 0.0)
            for g in range(2 * channels)
        ],
        axis=0,
    ).astype(jnp.bfloat16)
    scale = 1.0 / width.astype(jnp.float32)

    margin = (turned.shape[0] - all_pulses) // 2
    if whole_image:
        turned[0:margin, :] = jnp.zeros((margin, LANES), jnp.float32)
        turned[margin + all_pulses :, :] = jnp.zeros((margin, LANES), jnp.float32)
        azimuth_rows(filters_ref, tt, tt.shape[0] // (2 * filters_ref.shape[0]))

    pltpu.make_async_copy(send.at[pl.ds(0, n - 1)], recv.at[pl.ds(0, n - 1)], recv_sem).wait()

    for i in range(n):
        turned[margin + i * pulses : margin + (i + 1) * pulses, :] = recv[i].astype(jnp.float32)

    def corrected(start):
        taken = dot_nt(select, turned[start : start + LANES, :].astype(jnp.bfloat16))
        pulse = lane_id + (start - margin)
        weight = jnp.where((pulse >= low_edge) & (pulse < high_edge), scale, 0.0)
        return [taken[g * bins : (g + 1) * bins] * weight for g in range(2 * channels)]

    if whole_image:
        samples_out = filters_ref.shape[0]
        step = LANES // 2
        rows_in = jnp.concatenate(
            [jnp.concatenate(corrected(start), axis=1) for start in range(0, all_pulses, step)], axis=0
        ).astype(jnp.bfloat16)
        image = dot_nt(rows_in, tt[...])
        left = lane_id < step
        for s in range(samples_out):
            for b in range(all_pulses // LANES):
                at = 2 * b * bins
                early = image[at : at + bins, s * LANES : (s + 1) * LANES]
                late = image[at + bins : at + 2 * bins, s * LANES : (s + 1) * LANES]
                real = jnp.where(left, early, pltpu.roll(late, step, 1))
                imag = jnp.where(left, pltpu.roll(early, step, 1), late)
                out_ref[s, 0, :, b * LANES : (b + 1) * LANES] = real.astype(out_ref.dtype)
                out_ref[s, 1, :, b * LANES : (b + 1) * LANES] = imag.astype(out_ref.dtype)
    else:
        for b in range(all_pulses // LANES):
            for g, part in enumerate(corrected(b * LANES)):
                out_ref[g // 2, g % 2, :, b * LANES : (b + 1) * LANES] = part.astype(out_ref.dtype)

    pltpu.make_async_copy(send.at[pl.ds(0, n - 1)], recv.at[pl.ds(0, n - 1)], send_sem).wait()


def run_kernel(echoes, replica, recon_filters, span_offset, span_width, aperture_edges, whole_image):
    n = lax.axis_size("pulse")
    channels, pulses, _, samples = echoes.shape
    taps = replica.shape[1]
    bin_count = (samples - taps) // STEP
    bins = bin_count // n
    span = 2 * bins
    all_pulses = n * pulses
    blocks = bin_count // BLOCK
    group = min(blocks, 8)
    assert BLOCK % bins == 0 and channels * 2 * span == LANES and channels == BLOCK // bins
    assert blocks % group == 0 and all_pulses % LANES == 0
    depth = taps + 2 * LANES
    samples_out, _, _, az_taps = recon_filters.shape
    step = LANES // 2
    assert az_taps == step
    if whole_image:
        margin = az_taps // 2
        out_shape = (samples_out, 2, bins, all_pulses)
        tt_shape = (samples_out * 2 * step, channels * 2 * LANES)
    else:
        margin = 0
        out_shape = (channels, 2, bins, all_pulses)
        tt_shape = (16, LANES)
    operands = [
        pltpu.with_memory_space_constraint(array, pltpu.HBM)
        for array in (echoes, replica, recon_filters, span_offset, span_width, aperture_edges)
    ]
    vmem = pl.BlockSpec(memory_space=pltpu.VMEM)
    return pl.pallas_call(
        functools.partial(kernel, n, whole_image),
        out_shape=jax.ShapeDtypeStruct(out_shape, jnp.bfloat16),
        in_specs=[pl.BlockSpec(memory_space=pltpu.HBM)] * 6,
        out_specs=vmem,
        scratch_shapes=[
            pltpu.VMEM(replica.shape, jnp.bfloat16),
            pltpu.VMEM(recon_filters.shape, jnp.bfloat16),
            pltpu.SMEM(span_offset.shape, jnp.int32),
            pltpu.SMEM(span_width.shape, jnp.int32),
            pltpu.SMEM(aperture_edges.shape, jnp.int32),
            pltpu.VMEM((2 * channels * pulses, samples + LANES), jnp.bfloat16),
            pltpu.VMEM((2 * LANES, depth), jnp.bfloat16),
            pltpu.VMEM(tt_shape, jnp.bfloat16),
            pltpu.VMEM((2, channels, group * 2 * pulses, LANES), jnp.float32),
            pltpu.VMEM((n, pulses, LANES), jnp.bfloat16),
            pltpu.VMEM((n, pulses, LANES), jnp.bfloat16),
            pltpu.VMEM((all_pulses + 2 * margin, LANES), jnp.float32),
            pltpu.SemaphoreType.DMA((6,)),
            pltpu.SemaphoreType.DMA,
            pltpu.SemaphoreType.DMA,
        ],
        compiler_params=pltpu.CompilerParams(
            collective_id=0, has_side_effects=True, vmem_limit_bytes=32 * 1024 * 1024
        ),
    )(*operands)


def with_neighbours(cells, axis, dim, width):
    count = lax.axis_size(axis)
    head = lax.slice_in_dim(cells, 0, width, axis=dim)
    tail = lax.slice_in_dim(cells, cells.shape[dim] - width, cells.shape[dim], axis=dim)
    up = [(i, i + 1) for i in range(count - 1)]
    down = [(i + 1, i) for i in range(count - 1)]
    return jnp.concatenate(
        [lax.ppermute(tail, axis, up), cells, lax.ppermute(head, axis, down)], axis=dim
    )


def azimuth(padded, filters):
    channels, _, bin_count, padded_len = padded.shape
    subbands = filters.shape[0]
    tap_count = filters.shape[3]
    pulses = padded_len - tap_count
    span_len = tap_count + 4
    step_count = span_len // 4
    quartets = padded.reshape(channels, 2, bin_count, padded_len // 4, 4)
    window = jnp.stack(
        [quartets[:, :, :, first : first + pulses // 4, :] for first in range(step_count)], 4
    )
    window = window.transpose(2, 3, 0, 1, 4, 5).reshape(
        bin_count * (pulses // 4), channels * 2 * span_len
    )
    offset = jnp.arange(span_len)[:, None] - jnp.arange(4)[None, :]
    inside = (offset >= 0) & (offset < tap_count)
    picked = jnp.where(inside, jnp.take(filters, jnp.clip(offset, 0, tap_count - 1), axis=3), 0)
    real, imag = picked[:, :, 0], picked[:, :, 1]
    matrix = jnp.stack([jnp.stack([real, imag], 3), jnp.stack([-imag, real], 3)], 2)
    matrix = matrix.transpose(1, 2, 3, 0, 4, 5).reshape(channels * 2 * span_len, subbands * 8)
    result = jnp.dot(window, matrix, preferred_element_type=jnp.float32)
    result = result.reshape(bin_count, pulses // 4, subbands, 2, 4).transpose(2, 3, 0, 1, 4)
    return result.reshape(subbands, 2, bin_count, pulses)


def body(echoes, replica, recon_filters, span_offset, span_width, aperture_edges):
    operands = (echoes, replica, recon_filters, span_offset, span_width, aperture_edges)
    if lax.axis_size("chan") == 1 and echoes.shape[0] == recon_filters.shape[1]:
        return run_kernel(*operands, whole_image=True)
    corrected = run_kernel(*operands, whole_image=False)
    corrected = lax.all_to_all(corrected, "chan", split_axis=3, concat_axis=0, tiled=True)
    padded = with_neighbours(corrected, "chan", 3, recon_filters.shape[3] // 2)
    return azimuth(padded, recon_filters).astype(jnp.bfloat16)


def solution(mesh):
    return jax.shard_map(
        body,
        mesh=mesh,
        in_specs=(
            P("chan", "pulse", None, None),
            P(),
            P(),
            P("pulse"),
            P("pulse"),
            P(None, "pulse"),
        ),
        out_specs=P(None, None, "pulse", "chan"),
        check_vma=False,
    )
```

```python
import functools

import jax
import jax.numpy as jnp
from jax import lax
from jax.experimental import pallas as pl
from jax.experimental.pallas import tpu as pltpu
from jax.sharding import PartitionSpec as P

LANES = 128
STEP = 4
BLOCK = LANES // STEP
NT = (((1,), (1,)), ((), ()))


def dot_nt(a, b):
    return lax.dot_general(a, b, NT, preferred_element_type=jnp.float32)


def range_rows(replica_ref, bmat_ref, rows, depth):
    taps = replica_ref.shape[1]
    half = bmat_ref.shape[0] // 2
    filled = -(-rows // 16) * 16
    replica = replica_ref[...].astype(jnp.float32)
    for part in range(2):
        row = jnp.concatenate([replica[part : part + 1], jnp.zeros((1, depth - taps), jnp.float32)], axis=1)
        shifted = pltpu.roll(jnp.broadcast_to(row, (rows, depth)), 0, 1, stride=STEP, stride_axis=0)
        shifted = jnp.concatenate([shifted, jnp.zeros((filled - rows, depth), jnp.float32)], axis=0)
        bmat_ref[part * half : part * half + filled, :] = shifted.astype(jnp.bfloat16)


def azimuth_rows(filters_ref, tt_ref, step):
    samples, channels, _, taps = filters_ref.shape
    for s in range(samples):
        for c in range(channels):
            taps_row = filters_ref[s, c].astype(jnp.float32)
            taps_row = jnp.concatenate([taps_row, jnp.zeros((2, LANES - taps), jnp.float32)], axis=1)
            real, imag = [
                pltpu.roll(
                    jnp.broadcast_to(taps_row[part : part + 1], (step, LANES)), 0, 1, stride=1, stride_axis=0
                ).astype(jnp.bfloat16)
                for part in range(2)
            ]
            top, left = s * 2 * step, c * 2 * LANES
            tt_ref[top : top + step, left : left + LANES] = real
            tt_ref[top + step : top + 2 * step, left : left + LANES] = imag
            tt_ref[top : top + step, left + LANES : left + 2 * LANES] = -imag
            tt_ref[top + step : top + 2 * step, left + LANES : left + 2 * LANES] = real


def over_others(n):
    def run(step):
        if n <= 32:
            for k in range(1, n):
                step(k)
        else:
            pl.loop(1, n)(step)

    return run


def column(values, count):
    ids = lax.broadcasted_iota(jnp.int32, (count, LANES), 0)
    total = jnp.zeros((count, LANES), jnp.int32)
    for r in range(count):
        total = jnp.where(ids == r, values(r), total)
    return total


def kernel(
    n, whole_image,
    echoes_in, replica_in, filters_in, offset_in, width_in, edges_in,
    out_ref,
    replica_ref, filters_ref, offset_ref, width_ref, edges_ref,
    lines, bmat, tt, product, send, recv, turned,
    in_sem, send_sem, recv_sem,
):
    me = lax.axis_index("pulse")
    channels, pulses, _, samples = echoes_in.shape
    taps = replica_ref.shape[1]
    depth = bmat.shape[1]
    bin_count = (samples - taps) // STEP
    bins = bin_count // n
    span = 2 * bins
    windows = BLOCK // bins
    pairs = channels * pulses

    echo_rows = echoes_in.reshape(2 * pairs, samples)
    quarter = samples // 4
    quarters = [pl.ds(i * quarter, quarter) for i in range(4)]
    echoes_fetches = [
        pltpu.make_async_copy(echo_rows.at[:, at], lines.at[:, at], in_sem.at[5 + i])
        for i, at in enumerate(quarters)
    ]
    replica_fetch, *small_fetches = [
        pltpu.make_async_copy(source, held, in_sem.at[i])
        for i, (source, held) in enumerate(
            [
                (replica_in, replica_ref),
                (filters_in, filters_ref),
                (offset_in, offset_ref),
                (width_in, width_ref),
                (edges_in, edges_ref),
            ]
        )
    ]
    for fetch in [replica_fetch, *echoes_fetches, *small_fetches]:
        fetch.start()

    barrier = pltpu.get_barrier_semaphore()

    @over_others(n)
    def _(k):
        pl.semaphore_signal(
            barrier, inc=1, device_id={"pulse": jnp.where(me + k < n, me + k, me + k - n)}, device_id_type=pl.DeviceIdType.MESH
        )

    lines[:, samples:] = jnp.zeros((2 * pairs, lines.shape[1] - samples), lines.dtype)
    half = LANES // 2
    for part in range(2):
        bmat[(part + 1) * half - 16 : (part + 1) * half, :] = jnp.zeros((16, depth), bmat.dtype)
    replica_fetch.wait()
    range_rows(replica_ref, bmat, BLOCK + bins, depth)
    for fetch in echoes_fetches:
        fetch.wait()

    blocks = bin_count // BLOCK
    group = min(blocks, 8)
    rows = 2 * pulses
    lane = lax.broadcasted_iota(jnp.int32, (group * pulses, LANES), 1)
    for first in range(0, blocks, group):
        rows_in = jnp.concatenate(
            [lines[:, LANES * a : LANES * a + depth] for a in range(first, first + group)], axis=0
        )
        result = dot_nt(rows_in, bmat[...])
        for a in range(group):
            for c in range(channels):
                at = (a * channels + c) * rows
                product[c, a * rows : (a + 1) * rows, :] = result[at : at + rows]
        by_channel = []
        for c in range(channels):
            from_real = product[c, pl.ds(0, group * pulses, stride=2), :]
            from_imag = pltpu.roll(product[c, pl.ds(1, group * pulses, stride=2), :], half, 1)
            by_channel.append(jnp.where(lane < half, from_real - from_imag, from_real + from_imag))
        for w in range(windows):
            message = None
            for c in range(channels):
                shift = (span * c - bins * w) % LANES
                moved = pltpu.roll(by_channel[c], shift, 1) if shift else by_channel[c]
                message = moved if c == 0 else jnp.where(lane % half >= span * c, moved, message)
            for a in range(group):
                send[(first + a) * windows + w] = message[a * pulses : (a + 1) * pulses].astype(send.dtype)

    pl.semaphore_wait(barrier, n - 1)

    @over_others(n)
    def _(k):
        to = jnp.where(me + k < n, me + k, me + k - n)
        pltpu.make_async_remote_copy(
            src_ref=send.at[to], dst_ref=recv.at[me], send_sem=send_sem, recv_sem=recv_sem,
            device_id={"pulse": to}, device_id_type=pl.DeviceIdType.MESH,
        ).start()

    recv[me] = send[me]

    for fetch in small_fetches:
        fetch.wait()
    all_pulses = n * pulses
    row_id = lax.broadcasted_iota(jnp.int32, (bins, LANES), 0)
    lane_id = lax.broadcasted_iota(jnp.int32, (bins, LANES), 1)
    first_bin = row_id + column(lambda r: offset_ref[r], bins)
    width = column(lambda r: width_ref[r], bins)
    low_edge = column(lambda r: edges_ref[0, r], bins)
    high_edge = all_pulses - column(lambda r: edges_ref[1, r], bins)
    place = lane_id % span
    chosen = (place >= first_bin) & (place < first_bin + width) & (place + me * bins < bin_count)
    select = jnp.concatenate(
        [
            jnp.where(chosen & (lane_id // span == g % 2 * channels + g // 2), 1.0, 0.0)
            for g in range(2 * channels)
        ],
        axis=0,
    ).astype(jnp.bfloat16)
    scale = 1.0 / width.astype(jnp.float32)

    samples_out, _, _, az_taps = filters_ref.shape
    margin = az_taps // 2 if whole_image else 0
    if whole_image:
        step = tt.shape[0] // (2 * samples_out)
        after = turned.shape[0] - margin - all_pulses
        turned[0:margin, :] = jnp.zeros((margin, LANES), jnp.float32)
        turned[margin + all_pulses :, :] = jnp.zeros((after, LANES), jnp.float32)
        azimuth_rows(filters_ref, tt, step)

    pltpu.make_async_copy(send.at[pl.ds(0, n - 1)], recv.at[pl.ds(0, n - 1)], recv_sem).wait()

    for i in range(n):
        turned[margin + i * pulses : margin + (i + 1) * pulses, :] = recv[i].astype(jnp.float32)

    def corrected(start):
        taken = dot_nt(select, turned[start : start + LANES, :].astype(jnp.bfloat16))
        pulse = lane_id + (start - margin)
        weight = jnp.where((pulse >= low_edge) & (pulse < high_edge), scale, 0.0)
        return [taken[g * bins : (g + 1) * bins] * weight for g in range(2 * channels)]

    if whole_image:
        rows_in = jnp.concatenate(
            [jnp.concatenate(corrected(start), axis=1) for start in range(0, all_pulses, step)], axis=0
        ).astype(jnp.bfloat16)
        image = dot_nt(rows_in, tt[...])
        share = LANES // step
        for o in range(2 * samples_out):
            tile, at = o // share, o % share
            for b in range(all_pulses // LANES):
                joined = None
                for i in range(share):
                    top = (b * share + i) * bins
                    part = image[top : top + bins, tile * LANES : (tile + 1) * LANES]
                    shift = (i - at) * step % LANES
                    part = pltpu.roll(part, shift, 1) if shift else part
                    joined = part if i == 0 else jnp.where(lane_id >= i * step, part, joined)
                out_ref[o // 2, o % 2, :, b * LANES : (b + 1) * LANES] = joined.astype(out_ref.dtype)
    else:
        for b in range(all_pulses // LANES):
            for g, part in enumerate(corrected(b * LANES)):
                out_ref[g // 2, g % 2, :, b * LANES : (b + 1) * LANES] = part.astype(out_ref.dtype)

    pltpu.make_async_copy(send.at[pl.ds(0, n - 1)], recv.at[pl.ds(0, n - 1)], send_sem).wait()


def run_kernel(echoes, replica, recon_filters, span_offset, span_width, aperture_edges, whole_image):
    n = lax.axis_size("pulse")
    channels, pulses, _, samples = echoes.shape
    taps = replica.shape[1]
    bin_count = (samples - taps) // STEP
    bins = bin_count // n
    span = 2 * bins
    all_pulses = n * pulses
    blocks = bin_count // BLOCK
    group = min(blocks, 8)
    assert BLOCK % bins == 0 and channels * 2 * span == LANES
    assert BLOCK + bins <= LANES // 2 and samples % (4 * LANES) == 0
    assert blocks % group == 0 and all_pulses % LANES == 0
    depth = taps + 2 * LANES
    samples_out, _, _, az_taps = recon_filters.shape
    step = az_taps // 2
    assert az_taps + step <= LANES
    if whole_image:
        turned_rows = all_pulses - step + LANES
        out_shape = (samples_out, 2, bins, all_pulses)
        tt_shape = (samples_out * 2 * step, channels * 2 * LANES)
    else:
        turned_rows = all_pulses
        out_shape = (channels, 2, bins, all_pulses)
        tt_shape = (16, LANES)
    operands = [
        pltpu.with_memory_space_constraint(array, pltpu.HBM)
        for array in (echoes, replica, recon_filters, span_offset, span_width, aperture_edges)
    ]
    vmem = pl.BlockSpec(memory_space=pltpu.VMEM)
    return pl.pallas_call(
        functools.partial(kernel, n, whole_image),
        out_shape=jax.ShapeDtypeStruct(out_shape, jnp.bfloat16),
        in_specs=[pl.BlockSpec(memory_space=pltpu.HBM)] * 6,
        out_specs=vmem,
        scratch_shapes=[
            pltpu.VMEM(replica.shape, jnp.bfloat16),
            pltpu.VMEM(recon_filters.shape, jnp.bfloat16),
            pltpu.SMEM(span_offset.shape, jnp.int32),
            pltpu.SMEM(span_width.shape, jnp.int32),
            pltpu.SMEM(aperture_edges.shape, jnp.int32),
            pltpu.VMEM((2 * channels * pulses, samples + LANES), jnp.bfloat16),
            pltpu.VMEM((LANES, depth), jnp.bfloat16),
            pltpu.VMEM(tt_shape, jnp.bfloat16),
            pltpu.VMEM((channels, group * 2 * pulses, LANES), jnp.float32),
            pltpu.VMEM((n, pulses, LANES), jnp.bfloat16),
            pltpu.VMEM((n, pulses, LANES), jnp.bfloat16),
            pltpu.VMEM((turned_rows, LANES), jnp.float32),
            pltpu.SemaphoreType.DMA((9,)),
            pltpu.SemaphoreType.DMA,
            pltpu.SemaphoreType.DMA,
        ],
        compiler_params=pltpu.CompilerParams(
            collective_id=0, has_side_effects=True, vmem_limit_bytes=32 * 1024 * 1024
        ),
    )(*operands)


def with_neighbours(cells, axis, dim, width):
    count = lax.axis_size(axis)
    head = lax.slice_in_dim(cells, 0, width, axis=dim)
    tail = lax.slice_in_dim(cells, cells.shape[dim] - width, cells.shape[dim], axis=dim)
    up = [(i, i + 1) for i in range(count - 1)]
    down = [(i + 1, i) for i in range(count - 1)]
    return jnp.concatenate(
        [lax.ppermute(tail, axis, up), cells, lax.ppermute(head, axis, down)], axis=dim
    )


def azimuth(padded, filters):
    channels, _, bin_count, padded_len = padded.shape
    subbands = filters.shape[0]
    tap_count = filters.shape[3]
    pulses = padded_len - tap_count
    span_len = tap_count + 4
    step_count = span_len // 4
    quartets = padded.reshape(channels, 2, bin_count, padded_len // 4, 4)
    window = jnp.stack(
        [quartets[:, :, :, first : first + pulses // 4, :] for first in range(step_count)], 4
    )
    window = window.transpose(2, 3, 0, 1, 4, 5).reshape(
        bin_count * (pulses // 4), channels * 2 * span_len
    )
    offset = jnp.arange(span_len)[:, None] - jnp.arange(4)[None, :]
    inside = (offset >= 0) & (offset < tap_count)
    picked = jnp.where(inside, jnp.take(filters, jnp.clip(offset, 0, tap_count - 1), axis=3), 0)
    real, imag = picked[:, :, 0], picked[:, :, 1]
    matrix = jnp.stack([jnp.stack([real, imag], 3), jnp.stack([-imag, real], 3)], 2)
    matrix = matrix.transpose(1, 2, 3, 0, 4, 5).reshape(channels * 2 * span_len, subbands * 8)
    result = jnp.dot(window, matrix, preferred_element_type=jnp.float32)
    result = result.reshape(bin_count, pulses // 4, subbands, 2, 4).transpose(2, 3, 0, 1, 4)
    return result.reshape(subbands, 2, bin_count, pulses)


def body(echoes, replica, recon_filters, span_offset, span_width, aperture_edges):
    operands = (echoes, replica, recon_filters, span_offset, span_width, aperture_edges)
    if lax.axis_size("chan") == 1 and echoes.shape[0] == recon_filters.shape[1]:
        return run_kernel(*operands, whole_image=True)
    corrected = run_kernel(*operands, whole_image=False)
    corrected = lax.all_to_all(corrected, "chan", split_axis=3, concat_axis=0, tiled=True)
    padded = with_neighbours(corrected, "chan", 3, recon_filters.shape[3] // 2)
    return azimuth(padded, recon_filters).astype(jnp.bfloat16)


def solution(mesh):
    return jax.shard_map(
        body,
        mesh=mesh,
        in_specs=(
            P("chan", "pulse", None, None),
            P(),
            P(),
            P("pulse"),
            P("pulse"),
            P(None, "pulse"),
        ),
        out_specs=P(None, None, "pulse", "chan"),
        check_vma=False,
    )
```

```python
import functools

import jax
import jax.numpy as jnp
from jax import lax
from jax.experimental import pallas as pl
from jax.experimental.pallas import tpu as pltpu
from jax.sharding import PartitionSpec as P

LANES = 128
STEP = 4
BLOCK = LANES // STEP
NT = (((1,), (1,)), ((), ()))


def dot_nt(a, b):
    return lax.dot_general(a, b, NT, preferred_element_type=jnp.float32)


def range_rows(replica_ref, bmat_ref, rows, depth):
    taps = replica_ref.shape[1]
    half = bmat_ref.shape[0] // 2
    filled = -(-rows // 16) * 16
    replica = replica_ref[...].astype(jnp.float32)
    for part in range(2):
        row = jnp.concatenate([replica[part : part + 1], jnp.zeros((1, depth - taps), jnp.float32)], axis=1)
        shifted = pltpu.roll(jnp.broadcast_to(row, (rows, depth)), 0, 1, stride=STEP, stride_axis=0)
        shifted = jnp.concatenate([shifted, jnp.zeros((filled - rows, depth), jnp.float32)], axis=0)
        bmat_ref[part * half : part * half + filled, :] = shifted.astype(jnp.bfloat16)


def azimuth_rows(filters_ref, tt_ref, step):
    samples, channels, _, taps = filters_ref.shape
    for s in range(samples):
        for c in range(channels):
            taps_row = filters_ref[s, c].astype(jnp.float32)
            taps_row = jnp.concatenate([taps_row, jnp.zeros((2, LANES - taps), jnp.float32)], axis=1)
            real, imag = [
                pltpu.roll(
                    jnp.broadcast_to(taps_row[part : part + 1], (step, LANES)), 0, 1, stride=1, stride_axis=0
                ).astype(jnp.bfloat16)
                for part in range(2)
            ]
            top, left = s * 2 * step, c * 2 * LANES
            tt_ref[top : top + step, left : left + LANES] = real
            tt_ref[top + step : top + 2 * step, left : left + LANES] = imag
            tt_ref[top : top + step, left + LANES : left + 2 * LANES] = -imag
            tt_ref[top + step : top + 2 * step, left + LANES : left + 2 * LANES] = real


def over(first, last):
    def run(step):
        if last <= 32:
            for k in range(first, last):
                step(k)
        else:
            pl.loop(first, last)(step)

    return run


def column(values, count):
    ids = lax.broadcasted_iota(jnp.int32, (count, LANES), 0)
    total = jnp.zeros((count, LANES), jnp.int32)
    for r in range(count):
        total = jnp.where(ids == r, values(r), total)
    return total


def kernel(
    n, whole_image,
    echoes_in, replica_in, filters_in, offset_in, width_in, edges_in,
    out_ref,
    replica_ref, filters_ref, offset_ref, width_ref, edges_ref,
    lines, bmat, tt, product, send, recv, turned,
    in_sem, send_sem, recv_sem,
):
    me = lax.axis_index("pulse")
    channels, pulses, _, samples = echoes_in.shape
    taps = replica_ref.shape[1]
    depth = bmat.shape[1]
    bin_count = (samples - taps) // STEP
    bins = bin_count // n
    span = 2 * bins
    windows = BLOCK // bins
    pairs = channels * pulses

    echo_rows = echoes_in.reshape(2 * pairs, samples)
    quarter = samples // 4
    quarters = [pl.ds(i * quarter, quarter) for i in range(4)]
    echoes_fetches = [
        pltpu.make_async_copy(echo_rows.at[:, at], lines.at[:, at], in_sem.at[5 + i])
        for i, at in enumerate(quarters)
    ]
    replica_fetch, *small_fetches = [
        pltpu.make_async_copy(source, held, in_sem.at[i])
        for i, (source, held) in enumerate(
            [
                (replica_in, replica_ref),
                (filters_in, filters_ref),
                (offset_in, offset_ref),
                (width_in, width_ref),
                (edges_in, edges_ref),
            ]
        )
    ]
    for fetch in [replica_fetch, *echoes_fetches, *small_fetches]:
        fetch.start()

    barrier = pltpu.get_barrier_semaphore()

    @over(1, n)
    def _(k):
        pl.semaphore_signal(
            barrier, inc=1, device_id={"pulse": jnp.where(me + k < n, me + k, me + k - n)}, device_id_type=pl.DeviceIdType.MESH
        )

    lines[:, samples:] = jnp.zeros((2 * pairs, lines.shape[1] - samples), lines.dtype)
    half = LANES // 2
    for part in range(2):
        bmat[(part + 1) * half - 16 : (part + 1) * half, :] = jnp.zeros((16, depth), bmat.dtype)
    replica_fetch.wait()
    range_rows(replica_ref, bmat, BLOCK + bins, depth)
    for fetch in echoes_fetches:
        fetch.wait()

    group = product.shape[1] // (2 * pulses)
    groups = bin_count // BLOCK // group
    targets = group * windows
    rows = 2 * pulses
    lane = lax.broadcasted_iota(jnp.int32, (group * pulses, LANES), 1)
    for turn in range(groups):
        mine = me // targets
        chosen_group = mine + turn + 1
        chosen_group = jnp.where(chosen_group < groups, chosen_group, chosen_group - groups)
        rows_in = jnp.concatenate(
            [
                lines[:, pl.ds(pl.multiple_of(LANES * (chosen_group * group + a), LANES), depth)]
                for a in range(group)
            ],
            axis=0,
        )
        result = dot_nt(rows_in, bmat[...])
        for a in range(group):
            for c in range(channels):
                at = (a * channels + c) * rows
                product[c, a * rows : (a + 1) * rows, :] = result[at : at + rows]
        by_channel = []
        for c in range(channels):
            from_real = product[c, pl.ds(0, group * pulses, stride=2), :]
            from_imag = pltpu.roll(product[c, pl.ds(1, group * pulses, stride=2), :], half, 1)
            by_channel.append(jnp.where(lane < half, from_real - from_imag, from_real + from_imag))
        for w in range(windows):
            message = None
            for c in range(channels):
                shift = (span * c - bins * w) % LANES
                moved = pltpu.roll(by_channel[c], shift, 1) if shift else by_channel[c]
                message = moved if c == 0 else jnp.where(lane % half >= span * c, moved, message)
            for a in range(group):
                slot = (chosen_group * group + a) * windows + w
                send[slot] = message[a * pulses : (a + 1) * pulses].astype(send.dtype)

        if turn == 0:
            pl.semaphore_wait(barrier, n - 1)

        @over(int(turn == groups - 1), targets)
        def _(k):
            place = me - mine * targets + k
            to = chosen_group * targets + jnp.where(place < targets, place, place - targets)
            pltpu.make_async_remote_copy(
                src_ref=send.at[to], dst_ref=recv.at[me], send_sem=send_sem, recv_sem=recv_sem,
                device_id={"pulse": to}, device_id_type=pl.DeviceIdType.MESH,
            ).start()

    recv[me] = send[me]

    for fetch in small_fetches:
        fetch.wait()
    all_pulses = n * pulses
    row_id = lax.broadcasted_iota(jnp.int32, (bins, LANES), 0)
    lane_id = lax.broadcasted_iota(jnp.int32, (bins, LANES), 1)
    first_bin = row_id + column(lambda r: offset_ref[r], bins)
    width = column(lambda r: width_ref[r], bins)
    low_edge = column(lambda r: edges_ref[0, r], bins)
    high_edge = all_pulses - column(lambda r: edges_ref[1, r], bins)
    place = lane_id % span
    chosen = (place >= first_bin) & (place < first_bin + width) & (place + me * bins < bin_count)
    select = jnp.concatenate(
        [
            jnp.where(chosen & (lane_id // span == g % 2 * channels + g // 2), 1.0, 0.0)
            for g in range(2 * channels)
        ],
        axis=0,
    ).astype(jnp.bfloat16)
    scale = 1.0 / width.astype(jnp.float32)

    samples_out, _, _, az_taps = filters_ref.shape
    margin = az_taps // 2 if whole_image else 0
    if whole_image:
        step = tt.shape[0] // (2 * samples_out)
        after = turned.shape[0] - margin - all_pulses
        turned[0:margin, :] = jnp.zeros((margin, LANES), jnp.float32)
        turned[margin + all_pulses :, :] = jnp.zeros((after, LANES), jnp.float32)
        azimuth_rows(filters_ref, tt, step)

    pltpu.make_async_copy(send.at[pl.ds(0, n - 1)], recv.at[pl.ds(0, n - 1)], recv_sem).wait()

    for i in range(n):
        turned[margin + i * pulses : margin + (i + 1) * pulses, :] = recv[i].astype(jnp.float32)

    def corrected(start):
        taken = dot_nt(select, turned[start : start + LANES, :].astype(jnp.bfloat16))
        pulse = lane_id + (start - margin)
        weight = jnp.where((pulse >= low_edge) & (pulse < high_edge), scale, 0.0)
        return [taken[g * bins : (g + 1) * bins] * weight for g in range(2 * channels)]

    if whole_image:
        rows_in = jnp.concatenate(
            [jnp.concatenate(corrected(start), axis=1) for start in range(0, all_pulses, step)], axis=0
        ).astype(jnp.bfloat16)
        image = dot_nt(rows_in, tt[...])
        share = LANES // step
        for o in range(2 * samples_out):
            tile, at = o // share, o % share
            for b in range(all_pulses // LANES):
                joined = None
                for i in range(share):
                    top = (b * share + i) * bins
                    part = image[top : top + bins, tile * LANES : (tile + 1) * LANES]
                    shift = (i - at) * step % LANES
                    part = pltpu.roll(part, shift, 1) if shift else part
                    joined = part if i == 0 else jnp.where(lane_id >= i * step, part, joined)
                out_ref[o // 2, o % 2, :, b * LANES : (b + 1) * LANES] = joined.astype(out_ref.dtype)
    else:
        for b in range(all_pulses // LANES):
            for g, part in enumerate(corrected(b * LANES)):
                out_ref[g // 2, g % 2, :, b * LANES : (b + 1) * LANES] = part.astype(out_ref.dtype)

    pltpu.make_async_copy(send.at[pl.ds(0, n - 1)], recv.at[pl.ds(0, n - 1)], send_sem).wait()


def run_kernel(echoes, replica, recon_filters, span_offset, span_width, aperture_edges, whole_image):
    n = lax.axis_size("pulse")
    channels, pulses, _, samples = echoes.shape
    taps = replica.shape[1]
    bin_count = (samples - taps) // STEP
    bins = bin_count // n
    span = 2 * bins
    all_pulses = n * pulses
    blocks = bin_count // BLOCK
    group = max(4, blocks // 4)
    assert BLOCK % bins == 0 and channels * 2 * span == LANES
    assert BLOCK + bins <= LANES // 2 and samples % (4 * LANES) == 0
    assert blocks % group == 0 and all_pulses % LANES == 0
    depth = taps + 2 * LANES
    samples_out, _, _, az_taps = recon_filters.shape
    step = az_taps // 2
    assert az_taps + step <= LANES
    if whole_image:
        turned_rows = all_pulses - step + LANES
        out_shape = (samples_out, 2, bins, all_pulses)
        tt_shape = (samples_out * 2 * step, channels * 2 * LANES)
    else:
        turned_rows = all_pulses
        out_shape = (channels, 2, bins, all_pulses)
        tt_shape = (16, LANES)
    operands = [
        pltpu.with_memory_space_constraint(array, pltpu.HBM)
        for array in (echoes, replica, recon_filters, span_offset, span_width, aperture_edges)
    ]
    vmem = pl.BlockSpec(memory_space=pltpu.VMEM)
    return pl.pallas_call(
        functools.partial(kernel, n, whole_image),
        out_shape=jax.ShapeDtypeStruct(out_shape, jnp.bfloat16),
        in_specs=[pl.BlockSpec(memory_space=pltpu.HBM)] * 6,
        out_specs=vmem,
        scratch_shapes=[
            pltpu.VMEM(replica.shape, jnp.bfloat16),
            pltpu.VMEM(recon_filters.shape, jnp.bfloat16),
            pltpu.SMEM(span_offset.shape, jnp.int32),
            pltpu.SMEM(span_width.shape, jnp.int32),
            pltpu.SMEM(aperture_edges.shape, jnp.int32),
            pltpu.VMEM((2 * channels * pulses, samples + LANES), jnp.bfloat16),
            pltpu.VMEM((LANES, depth), jnp.bfloat16),
            pltpu.VMEM(tt_shape, jnp.bfloat16),
            pltpu.VMEM((channels, group * 2 * pulses, LANES), jnp.float32),
            pltpu.VMEM((n, pulses, LANES), jnp.bfloat16),
            pltpu.VMEM((n, pulses, LANES), jnp.bfloat16),
            pltpu.VMEM((turned_rows, LANES), jnp.float32),
            pltpu.SemaphoreType.DMA((9,)),
            pltpu.SemaphoreType.DMA,
            pltpu.SemaphoreType.DMA,
        ],
        compiler_params=pltpu.CompilerParams(
            collective_id=0, has_side_effects=True, vmem_limit_bytes=32 * 1024 * 1024
        ),
    )(*operands)


def with_neighbours(cells, axis, dim, width):
    count = lax.axis_size(axis)
    head = lax.slice_in_dim(cells, 0, width, axis=dim)
    tail = lax.slice_in_dim(cells, cells.shape[dim] - width, cells.shape[dim], axis=dim)
    up = [(i, i + 1) for i in range(count - 1)]
    down = [(i + 1, i) for i in range(count - 1)]
    return jnp.concatenate(
        [lax.ppermute(tail, axis, up), cells, lax.ppermute(head, axis, down)], axis=dim
    )


def azimuth(padded, filters):
    channels, _, bin_count, padded_len = padded.shape
    subbands = filters.shape[0]
    tap_count = filters.shape[3]
    pulses = padded_len - tap_count
    span_len = tap_count + 4
    step_count = span_len // 4
    quartets = padded.reshape(channels, 2, bin_count, padded_len // 4, 4)
    window = jnp.stack(
        [quartets[:, :, :, first : first + pulses // 4, :] for first in range(step_count)], 4
    )
    window = window.transpose(2, 3, 0, 1, 4, 5).reshape(
        bin_count * (pulses // 4), channels * 2 * span_len
    )
    offset = jnp.arange(span_len)[:, None] - jnp.arange(4)[None, :]
    inside = (offset >= 0) & (offset < tap_count)
    picked = jnp.where(inside, jnp.take(filters, jnp.clip(offset, 0, tap_count - 1), axis=3), 0)
    real, imag = picked[:, :, 0], picked[:, :, 1]
    matrix = jnp.stack([jnp.stack([real, imag], 3), jnp.stack([-imag, real], 3)], 2)
    matrix = matrix.transpose(1, 2, 3, 0, 4, 5).reshape(channels * 2 * span_len, subbands * 8)
    result = jnp.dot(window, matrix, preferred_element_type=jnp.float32)
    result = result.reshape(bin_count, pulses // 4, subbands, 2, 4).transpose(2, 3, 0, 1, 4)
    return result.reshape(subbands, 2, bin_count, pulses)


def body(echoes, replica, recon_filters, span_offset, span_width, aperture_edges):
    operands = (echoes, replica, recon_filters, span_offset, span_width, aperture_edges)
    if lax.axis_size("chan") == 1 and echoes.shape[0] == recon_filters.shape[1]:
        return run_kernel(*operands, whole_image=True)
    corrected = run_kernel(*operands, whole_image=False)
    corrected = lax.all_to_all(corrected, "chan", split_axis=3, concat_axis=0, tiled=True)
    padded = with_neighbours(corrected, "chan", 3, recon_filters.shape[3] // 2)
    return azimuth(padded, recon_filters).astype(jnp.bfloat16)


def solution(mesh):
    return jax.shard_map(
        body,
        mesh=mesh,
        in_specs=(
            P("chan", "pulse", None, None),
            P(),
            P(),
            P("pulse"),
            P("pulse"),
            P(None, "pulse"),
        ),
        out_specs=P(None, None, "pulse", "chan"),
        check_vma=False,
    )
```

```python
import functools

import jax
import jax.numpy as jnp
from jax import lax
from jax.experimental import pallas as pl
from jax.experimental.pallas import tpu as pltpu
from jax.sharding import PartitionSpec as P

LANES = 128
STEP = 4
BLOCK = LANES // STEP
NT = (((1,), (1,)), ((), ()))


def dot_nt(a, b):
    return lax.dot_general(a, b, NT, preferred_element_type=jnp.float32)


def range_rows(replica_ref, bmat_ref, rows, depth):
    taps = replica_ref.shape[1]
    half = bmat_ref.shape[0] // 2
    filled = -(-rows // 16) * 16
    replica = replica_ref[...].astype(jnp.float32)
    for part in range(2):
        row = jnp.concatenate([replica[part : part + 1], jnp.zeros((1, depth - taps), jnp.float32)], axis=1)
        shifted = pltpu.roll(jnp.broadcast_to(row, (rows, depth)), 0, 1, stride=STEP, stride_axis=0)
        shifted = jnp.concatenate([shifted, jnp.zeros((filled - rows, depth), jnp.float32)], axis=0)
        bmat_ref[part * half : part * half + filled, :] = shifted.astype(jnp.bfloat16)


def azimuth_rows(filters_ref, tt_ref, step):
    samples, channels, _, taps = filters_ref.shape
    for s in range(samples):
        for c in range(channels):
            taps_row = filters_ref[s, c].astype(jnp.float32)
            taps_row = jnp.concatenate([taps_row, jnp.zeros((2, LANES - taps), jnp.float32)], axis=1)
            real, imag = [
                pltpu.roll(
                    jnp.broadcast_to(taps_row[part : part + 1], (step, LANES)), 0, 1, stride=1, stride_axis=0
                ).astype(jnp.bfloat16)
                for part in range(2)
            ]
            top, left = s * 2 * step, c * 2 * LANES
            tt_ref[top : top + step, left : left + LANES] = real
            tt_ref[top + step : top + 2 * step, left : left + LANES] = imag
            tt_ref[top : top + step, left + LANES : left + 2 * LANES] = -imag
            tt_ref[top + step : top + 2 * step, left + LANES : left + 2 * LANES] = real


def over(first, last):
    def run(step):
        if last <= 32:
            for k in range(first, last):
                step(k)
        else:
            pl.loop(first, last)(step)

    return run


def column(values, count):
    ids = lax.broadcasted_iota(jnp.int32, (count, LANES), 0)
    total = jnp.zeros((count, LANES), jnp.int32)
    for r in range(count):
        total = jnp.where(ids == r, values(r), total)
    return total


def kernel(
    n, whole_image,
    echoes_in, replica_in, filters_in, offset_in, width_in, edges_in,
    out_ref,
    replica_ref, filters_ref, offset_ref, width_ref, edges_ref,
    lines, bmat, tt, product, send, recv, turned,
    in_sem, send_sem, recv_sem,
):
    me = lax.axis_index("pulse")
    channels, pulses, _, samples = echoes_in.shape
    taps = replica_ref.shape[1]
    depth = bmat.shape[1]
    bin_count = (samples - taps) // STEP
    bins = bin_count // n
    span = 2 * bins
    windows = BLOCK // bins
    pairs = channels * pulses

    echo_rows = echoes_in.reshape(2 * pairs, samples)
    share = samples // 8
    shares = [pl.ds(i * share, share) for i in range(8)]
    echoes_fetches = [
        pltpu.make_async_copy(echo_rows.at[:, at], lines.at[:, at], in_sem.at[5 + i])
        for i, at in enumerate(shares)
    ]
    replica_fetch, *small_fetches = [
        pltpu.make_async_copy(source, held, in_sem.at[i])
        for i, (source, held) in enumerate(
            [
                (replica_in, replica_ref),
                (filters_in, filters_ref),
                (offset_in, offset_ref),
                (width_in, width_ref),
                (edges_in, edges_ref),
            ]
        )
    ]
    for fetch in [replica_fetch, *echoes_fetches, *small_fetches]:
        fetch.start()

    barrier = pltpu.get_barrier_semaphore()

    @over(1, n)
    def _(k):
        pl.semaphore_signal(
            barrier, inc=1, device_id={"pulse": jnp.where(me + k < n, me + k, me + k - n)}, device_id_type=pl.DeviceIdType.MESH
        )

    lines[:, samples:] = jnp.zeros((2 * pairs, lines.shape[1] - samples), lines.dtype)
    half = LANES // 2
    for part in range(2):
        bmat[(part + 1) * half - 16 : (part + 1) * half, :] = jnp.zeros((16, depth), bmat.dtype)
    replica_fetch.wait()
    range_rows(replica_ref, bmat, BLOCK + bins, depth)
    for fetch in echoes_fetches:
        fetch.wait()

    group = product.shape[1] // (2 * pulses)
    groups = bin_count // BLOCK // group
    targets = group * windows
    rows = 2 * pulses
    lane = lax.broadcasted_iota(jnp.int32, (group * pulses, LANES), 1)
    for turn in range(groups):
        rows_in = jnp.concatenate(
            [
                lines[:, LANES * (turn * group + a) : LANES * (turn * group + a) + depth]
                for a in range(group)
            ],
            axis=0,
        )
        result = dot_nt(rows_in, bmat[...])
        for a in range(group):
            for c in range(channels):
                at = (a * channels + c) * rows
                product[c, a * rows : (a + 1) * rows, :] = result[at : at + rows]
        by_channel = []
        for c in range(channels):
            from_real = product[c, pl.ds(0, group * pulses, stride=2), :]
            from_imag = pltpu.roll(product[c, pl.ds(1, group * pulses, stride=2), :], half, 1)
            by_channel.append(jnp.where(lane < half, from_real - from_imag, from_real + from_imag))
        for w in range(windows):
            message = None
            for c in range(channels):
                shift = (span * c - bins * w) % LANES
                moved = pltpu.roll(by_channel[c], shift, 1) if shift else by_channel[c]
                message = moved if c == 0 else jnp.where(lane % half >= span * c, moved, message)
            for a in range(group):
                slot = (turn * group + a) * windows + w
                send[slot] = message[a * pulses : (a + 1) * pulses].astype(send.dtype)

        if turn == 0:
            pl.semaphore_wait(barrier, n - 1)

        ahead = 2 if turn == 0 else 0
        others = targets - ahead

        def send_to(to):
            @pl.when(to != me)
            def _():
                pltpu.make_async_remote_copy(
                    src_ref=send.at[to], dst_ref=recv.at[me], send_sem=send_sem, recv_sem=recv_sem,
                    device_id={"pulse": to}, device_id_type=pl.DeviceIdType.MESH,
                ).start()

        for to in range(ahead):
            send_to(to)
        begin = lax.rem(me, others)

        @over(0, others)
        def _(k):
            place = begin + k
            send_to(turn * targets + ahead + jnp.where(place < others, place, place - others))

    recv[me] = send[me]

    for fetch in small_fetches:
        fetch.wait()
    all_pulses = n * pulses
    row_id = lax.broadcasted_iota(jnp.int32, (bins, LANES), 0)
    lane_id = lax.broadcasted_iota(jnp.int32, (bins, LANES), 1)
    first_bin = row_id + column(lambda r: offset_ref[r], bins)
    width = column(lambda r: width_ref[r], bins)
    low_edge = column(lambda r: edges_ref[0, r], bins)
    high_edge = all_pulses - column(lambda r: edges_ref[1, r], bins)
    place = lane_id % span
    chosen = (place >= first_bin) & (place < first_bin + width) & (place + me * bins < bin_count)
    select = jnp.concatenate(
        [
            jnp.where(chosen & (lane_id // span == g % 2 * channels + g // 2), 1.0, 0.0)
            for g in range(2 * channels)
        ],
        axis=0,
    ).astype(jnp.bfloat16)
    scale = 1.0 / width.astype(jnp.float32)

    samples_out, _, _, az_taps = filters_ref.shape
    margin = az_taps // 2 if whole_image else 0
    step = tt.shape[0] // (2 * samples_out) if whole_image else LANES
    weights = {}
    for start in range(0, all_pulses, step):
        pulse = lane_id + (start - margin)
        weights[start] = jnp.where((pulse >= low_edge) & (pulse < high_edge), scale, 0.0)
    if whole_image:
        after = turned.shape[0] - margin - all_pulses
        turned[0:margin, :] = jnp.zeros((margin, LANES), jnp.float32)
        turned[margin + all_pulses :, :] = jnp.zeros((after, LANES), jnp.float32)
        azimuth_rows(filters_ref, tt, step)

    pltpu.make_async_copy(send.at[pl.ds(0, n - 1)], recv.at[pl.ds(0, n - 1)], recv_sem).wait()

    for i in range(n):
        turned[margin + i * pulses : margin + (i + 1) * pulses, :] = recv[i].astype(jnp.float32)

    def corrected(start):
        taken = dot_nt(select, turned[start : start + LANES, :].astype(jnp.bfloat16))
        return [taken[g * bins : (g + 1) * bins] * weights[start] for g in range(2 * channels)]

    if whole_image:
        rows_in = jnp.concatenate(
            [jnp.concatenate(corrected(start), axis=1) for start in range(0, all_pulses, step)], axis=0
        ).astype(jnp.bfloat16)
        image = dot_nt(rows_in, tt[...])
        share = LANES // step
        for o in range(2 * samples_out):
            tile, at = o // share, o % share
            for b in range(all_pulses // LANES):
                joined = None
                for i in range(share):
                    top = (b * share + i) * bins
                    part = image[top : top + bins, tile * LANES : (tile + 1) * LANES]
                    shift = (i - at) * step % LANES
                    part = pltpu.roll(part, shift, 1) if shift else part
                    joined = part if i == 0 else jnp.where(lane_id >= i * step, part, joined)
                out_ref[o // 2, o % 2, :, b * LANES : (b + 1) * LANES] = joined.astype(out_ref.dtype)
    else:
        for b in range(all_pulses // LANES):
            for g, part in enumerate(corrected(b * LANES)):
                out_ref[g // 2, g % 2, :, b * LANES : (b + 1) * LANES] = part.astype(out_ref.dtype)

    pltpu.make_async_copy(send.at[pl.ds(0, n - 1)], recv.at[pl.ds(0, n - 1)], send_sem).wait()


def run_kernel(echoes, replica, recon_filters, span_offset, span_width, aperture_edges, whole_image):
    n = lax.axis_size("pulse")
    channels, pulses, _, samples = echoes.shape
    taps = replica.shape[1]
    bin_count = (samples - taps) // STEP
    bins = bin_count // n
    span = 2 * bins
    all_pulses = n * pulses
    blocks = bin_count // BLOCK
    group = max(4, blocks // 4)
    assert BLOCK % bins == 0 and channels * 2 * span == LANES
    assert BLOCK + bins <= LANES // 2 and samples % (8 * LANES) == 0
    assert blocks % group == 0 and all_pulses % LANES == 0
    depth = taps + 2 * LANES
    samples_out, _, _, az_taps = recon_filters.shape
    step = az_taps // 2
    assert az_taps + step <= LANES
    if whole_image:
        turned_rows = all_pulses - step + LANES
        out_shape = (samples_out, 2, bins, all_pulses)
        tt_shape = (samples_out * 2 * step, channels * 2 * LANES)
    else:
        turned_rows = all_pulses
        out_shape = (channels, 2, bins, all_pulses)
        tt_shape = (16, LANES)
    operands = [
        pltpu.with_memory_space_constraint(array, pltpu.HBM)
        for array in (echoes, replica, recon_filters, span_offset, span_width, aperture_edges)
    ]
    vmem = pl.BlockSpec(memory_space=pltpu.VMEM)
    return pl.pallas_call(
        functools.partial(kernel, n, whole_image),
        out_shape=jax.ShapeDtypeStruct(out_shape, jnp.bfloat16),
        in_specs=[pl.BlockSpec(memory_space=pltpu.HBM)] * 6,
        out_specs=vmem,
        scratch_shapes=[
            pltpu.VMEM(replica.shape, jnp.bfloat16),
            pltpu.VMEM(recon_filters.shape, jnp.bfloat16),
            pltpu.SMEM(span_offset.shape, jnp.int32),
            pltpu.SMEM(span_width.shape, jnp.int32),
            pltpu.SMEM(aperture_edges.shape, jnp.int32),
            pltpu.VMEM((2 * channels * pulses, samples + LANES), jnp.bfloat16),
            pltpu.VMEM((LANES, depth), jnp.bfloat16),
            pltpu.VMEM(tt_shape, jnp.bfloat16),
            pltpu.VMEM((channels, group * 2 * pulses, LANES), jnp.float32),
            pltpu.VMEM((n, pulses, LANES), jnp.bfloat16),
            pltpu.VMEM((n, pulses, LANES), jnp.bfloat16),
            pltpu.VMEM((turned_rows, LANES), jnp.float32),
            pltpu.SemaphoreType.DMA((13,)),
            pltpu.SemaphoreType.DMA,
            pltpu.SemaphoreType.DMA,
        ],
        compiler_params=pltpu.CompilerParams(
            collective_id=0, has_side_effects=True, vmem_limit_bytes=32 * 1024 * 1024
        ),
    )(*operands)


def with_neighbours(cells, axis, dim, width):
    count = lax.axis_size(axis)
    head = lax.slice_in_dim(cells, 0, width, axis=dim)
    tail = lax.slice_in_dim(cells, cells.shape[dim] - width, cells.shape[dim], axis=dim)
    up = [(i, i + 1) for i in range(count - 1)]
    down = [(i + 1, i) for i in range(count - 1)]
    return jnp.concatenate(
        [lax.ppermute(tail, axis, up), cells, lax.ppermute(head, axis, down)], axis=dim
    )


def azimuth(padded, filters):
    channels, _, bin_count, padded_len = padded.shape
    subbands = filters.shape[0]
    tap_count = filters.shape[3]
    pulses = padded_len - tap_count
    span_len = tap_count + 4
    step_count = span_len // 4
    quartets = padded.reshape(channels, 2, bin_count, padded_len // 4, 4)
    window = jnp.stack(
        [quartets[:, :, :, first : first + pulses // 4, :] for first in range(step_count)], 4
    )
    window = window.transpose(2, 3, 0, 1, 4, 5).reshape(
        bin_count * (pulses // 4), channels * 2 * span_len
    )
    offset = jnp.arange(span_len)[:, None] - jnp.arange(4)[None, :]
    inside = (offset >= 0) & (offset < tap_count)
    picked = jnp.where(inside, jnp.take(filters, jnp.clip(offset, 0, tap_count - 1), axis=3), 0)
    real, imag = picked[:, :, 0], picked[:, :, 1]
    matrix = jnp.stack([jnp.stack([real, imag], 3), jnp.stack([-imag, real], 3)], 2)
    matrix = matrix.transpose(1, 2, 3, 0, 4, 5).reshape(channels * 2 * span_len, subbands * 8)
    result = jnp.dot(window, matrix, preferred_element_type=jnp.float32)
    result = result.reshape(bin_count, pulses // 4, subbands, 2, 4).transpose(2, 3, 0, 1, 4)
    return result.reshape(subbands, 2, bin_count, pulses)


def body(echoes, replica, recon_filters, span_offset, span_width, aperture_edges):
    operands = (echoes, replica, recon_filters, span_offset, span_width, aperture_edges)
    if lax.axis_size("chan") == 1 and echoes.shape[0] == recon_filters.shape[1]:
        return run_kernel(*operands, whole_image=True)
    corrected = run_kernel(*operands, whole_image=False)
    corrected = lax.all_to_all(corrected, "chan", split_axis=3, concat_axis=0, tiled=True)
    padded = with_neighbours(corrected, "chan", 3, recon_filters.shape[3] // 2)
    return azimuth(padded, recon_filters).astype(jnp.bfloat16)


def solution(mesh):
    return jax.shard_map(
        body,
        mesh=mesh,
        in_specs=(
            P("chan", "pulse", None, None),
            P(),
            P(),
            P("pulse"),
            P("pulse"),
            P(None, "pulse"),
        ),
        out_specs=P(None, None, "pulse", "chan"),
        check_vma=False,
    )
```

```python
import functools

import jax
import jax.numpy as jnp
from jax import lax
from jax.experimental import pallas as pl
from jax.experimental.pallas import tpu as pltpu
from jax.sharding import PartitionSpec as P

LANES = 128
STEP = 4
BLOCK = LANES // STEP
NT = (((1,), (1,)), ((), ()))


def dot_nt(a, b):
    return lax.dot_general(a, b, NT, preferred_element_type=jnp.float32)


def range_rows(replica_ref, bmat_ref, rows, depth):
    taps = replica_ref.shape[1]
    half = bmat_ref.shape[0] // 2
    filled = -(-rows // 16) * 16
    replica = replica_ref[...].astype(jnp.float32)
    for part in range(2):
        row = jnp.concatenate([replica[part : part + 1], jnp.zeros((1, depth - taps), jnp.float32)], axis=1)
        shifted = pltpu.roll(jnp.broadcast_to(row, (rows, depth)), 0, 1, stride=STEP, stride_axis=0)
        shifted = jnp.concatenate([shifted, jnp.zeros((filled - rows, depth), jnp.float32)], axis=0)
        bmat_ref[part * half : part * half + filled, :] = shifted.astype(jnp.bfloat16)


def azimuth_rows(filters_ref, tt_ref, step):
    samples, channels, _, taps = filters_ref.shape
    for s in range(samples):
        for c in range(channels):
            taps_row = filters_ref[s, c].astype(jnp.float32)
            taps_row = jnp.concatenate([taps_row, jnp.zeros((2, LANES - taps), jnp.float32)], axis=1)
            real, imag = [
                pltpu.roll(
                    jnp.broadcast_to(taps_row[part : part + 1], (step, LANES)), 0, 1, stride=1, stride_axis=0
                ).astype(jnp.bfloat16)
                for part in range(2)
            ]
            top, left = s * 2 * step, c * 2 * LANES
            tt_ref[top : top + step, left : left + LANES] = real
            tt_ref[top + step : top + 2 * step, left : left + LANES] = imag
            tt_ref[top : top + step, left + LANES : left + 2 * LANES] = -imag
            tt_ref[top + step : top + 2 * step, left + LANES : left + 2 * LANES] = real


def over(first, last):
    def run(step):
        if last <= 32:
            for k in range(first, last):
                step(k)
        else:
            pl.loop(first, last)(step)

    return run


def column(values, count):
    ids = lax.broadcasted_iota(jnp.int32, (count, LANES), 0)
    total = jnp.zeros((count, LANES), jnp.int32)
    for r in range(count):
        total = jnp.where(ids == r, values(r), total)
    return total


def kernel(
    n, whole_image,
    echoes_in, replica_in, filters_in, offset_in, width_in, edges_in,
    out_ref,
    replica_ref, filters_ref, offset_ref, width_ref, edges_ref,
    lines, bmat, tt, select, weights, product, send, recv, turned,
    in_sem, send_sem, recv_sem,
):
    me = lax.axis_index("pulse")
    channels, pulses, _, samples = echoes_in.shape
    taps = replica_ref.shape[1]
    depth = bmat.shape[1]
    bin_count = (samples - taps) // STEP
    bins = bin_count // n
    span = 2 * bins
    windows = BLOCK // bins
    pairs = channels * pulses

    echo_rows = echoes_in.reshape(2 * pairs, samples)
    share = samples // 8
    shares = [pl.ds(i * share, share) for i in range(8)]
    echoes_fetches = [
        pltpu.make_async_copy(echo_rows.at[:, at], lines.at[:, at], in_sem.at[5 + i])
        for i, at in enumerate(shares)
    ]
    replica_fetch, *small_fetches = [
        pltpu.make_async_copy(source, held, in_sem.at[i])
        for i, (source, held) in enumerate(
            [
                (replica_in, replica_ref),
                (filters_in, filters_ref),
                (offset_in, offset_ref),
                (width_in, width_ref),
                (edges_in, edges_ref),
            ]
        )
    ]
    for fetch in [replica_fetch, *echoes_fetches, *small_fetches]:
        fetch.start()

    barrier = pltpu.get_barrier_semaphore()

    @over(1, n)
    def _(k):
        pl.semaphore_signal(
            barrier, inc=1, device_id={"pulse": jnp.where(me + k < n, me + k, me + k - n)}, device_id_type=pl.DeviceIdType.MESH
        )

    lines[:, samples:] = jnp.zeros((2 * pairs, lines.shape[1] - samples), lines.dtype)
    half = LANES // 2
    for part in range(2):
        bmat[(part + 1) * half - 16 : (part + 1) * half, :] = jnp.zeros((16, depth), bmat.dtype)
    replica_fetch.wait()
    range_rows(replica_ref, bmat, BLOCK + bins, depth)
    for fetch in echoes_fetches:
        fetch.wait()

    all_pulses = n * pulses
    samples_out, _, _, az_taps = filters_ref.shape
    margin = az_taps // 2 if whole_image else 0
    step = tt.shape[0] // (2 * samples_out) if whole_image else LANES
    lane_id = lax.broadcasted_iota(jnp.int32, (bins, LANES), 1)

    def prepare():
        for fetch in small_fetches:
            fetch.wait()
        row_id = lax.broadcasted_iota(jnp.int32, (bins, LANES), 0)
        first_bin = row_id + column(lambda r: offset_ref[r], bins)
        width = column(lambda r: width_ref[r], bins)
        low_edge = column(lambda r: edges_ref[0, r], bins)
        high_edge = all_pulses - column(lambda r: edges_ref[1, r], bins)
        place = lane_id % span
        chosen = (place >= first_bin) & (place < first_bin + width) & (place + me * bins < bin_count)
        select[...] = jnp.concatenate(
            [
                jnp.where(chosen & (lane_id // span == g % 2 * channels + g // 2), 1.0, 0.0)
                for g in range(2 * channels)
            ],
            axis=0,
        ).astype(jnp.bfloat16)
        scale = 1.0 / width.astype(jnp.float32)

        for i, start in enumerate(range(0, all_pulses, step)):
            pulse = lane_id + (start - margin)
            weights[i * bins : (i + 1) * bins, :] = jnp.where((pulse >= low_edge) & (pulse < high_edge), scale, 0.0)
        if whole_image:
            after = turned.shape[0] - margin - all_pulses
            turned[0:margin, :] = jnp.zeros((margin, LANES), jnp.float32)
            turned[margin + all_pulses :, :] = jnp.zeros((after, LANES), jnp.float32)
            azimuth_rows(filters_ref, tt, step)

    group = product.shape[1] // (2 * pulses)
    groups = bin_count // BLOCK // group
    targets = group * windows
    rows = 2 * pulses
    lane = lax.broadcasted_iota(jnp.int32, (group * pulses, LANES), 1)
    ahead = 2
    first_here = me < ahead

    def send_to(to):
        @pl.when(to != me)
        def _():
            pltpu.make_async_remote_copy(
                src_ref=send.at[to], dst_ref=recv.at[me], send_sem=send_sem, recv_sem=recv_sem,
                device_id={"pulse": to}, device_id_type=pl.DeviceIdType.MESH,
            ).start()

    def send_group(turn):
        served = ahead if turn == 0 else 0
        others = targets - served
        for to in range(served):
            send_to(to)
        begin = lax.rem(me, others)

        @over(0, others)
        def _(k):
            place = begin + k
            send_to(turn * targets + served + jnp.where(place < others, place, place - others))

    for turn in range(groups):
        rows_in = jnp.concatenate(
            [
                lines[:, LANES * (turn * group + a) : LANES * (turn * group + a) + depth]
                for a in range(group)
            ],
            axis=0,
        )
        result = dot_nt(rows_in, bmat[...])
        for a in range(group):
            for c in range(channels):
                at = (a * channels + c) * rows
                product[c, a * rows : (a + 1) * rows, :] = result[at : at + rows]
        by_channel = []
        for c in range(channels):
            from_real = product[c, pl.ds(0, group * pulses, stride=2), :]
            from_imag = pltpu.roll(product[c, pl.ds(1, group * pulses, stride=2), :], half, 1)
            by_channel.append(jnp.where(lane < half, from_real - from_imag, from_real + from_imag))
        for w in range(windows):
            message = None
            for c in range(channels):
                shift = (span * c - bins * w) % LANES
                moved = pltpu.roll(by_channel[c], shift, 1) if shift else by_channel[c]
                message = moved if c == 0 else jnp.where(lane % half >= span * c, moved, message)
            for a in range(group):
                slot = (turn * group + a) * windows + w
                send[slot] = message[a * pulses : (a + 1) * pulses].astype(send.dtype)

        if turn == groups - 1:

            @pl.when(first_here)
            def _():
                prepare()
                pl.semaphore_wait(barrier, n - 1)
                for before in range(turn):
                    send_group(before)

            send_group(turn)
        else:

            @pl.when(jnp.logical_not(first_here))
            def _():
                if turn == 0:
                    pl.semaphore_wait(barrier, n - 1)
                send_group(turn)

    pl.when(jnp.logical_not(first_here))(prepare)
    recv[me] = send[me]

    pltpu.make_async_copy(send.at[pl.ds(0, n - 1)], recv.at[pl.ds(0, n - 1)], recv_sem).wait()

    for i in range(n):
        turned[margin + i * pulses : margin + (i + 1) * pulses, :] = recv[i].astype(jnp.float32)

    def corrected(start):
        taken = dot_nt(select[...], turned[start : start + LANES, :].astype(jnp.bfloat16))
        at = start // step * bins
        weight = weights[at : at + bins]
        return [taken[g * bins : (g + 1) * bins] * weight for g in range(2 * channels)]

    if whole_image:
        rows_in = jnp.concatenate(
            [jnp.concatenate(corrected(start), axis=1) for start in range(0, all_pulses, step)], axis=0
        ).astype(jnp.bfloat16)
        image = dot_nt(rows_in, tt[...])
        share = LANES // step
        for o in range(2 * samples_out):
            tile, at = o // share, o % share
            for b in range(all_pulses // LANES):
                joined = None
                for i in range(share):
                    top = (b * share + i) * bins
                    part = image[top : top + bins, tile * LANES : (tile + 1) * LANES]
                    shift = (i - at) * step % LANES
                    part = pltpu.roll(part, shift, 1) if shift else part
                    joined = part if i == 0 else jnp.where(lane_id >= i * step, part, joined)
                out_ref[o // 2, o % 2, :, b * LANES : (b + 1) * LANES] = joined.astype(out_ref.dtype)
    else:
        for b in range(all_pulses // LANES):
            for g, part in enumerate(corrected(b * LANES)):
                out_ref[g // 2, g % 2, :, b * LANES : (b + 1) * LANES] = part.astype(out_ref.dtype)

    pltpu.make_async_copy(send.at[pl.ds(0, n - 1)], recv.at[pl.ds(0, n - 1)], send_sem).wait()


def run_kernel(echoes, replica, recon_filters, span_offset, span_width, aperture_edges, whole_image):
    n = lax.axis_size("pulse")
    channels, pulses, _, samples = echoes.shape
    taps = replica.shape[1]
    bin_count = (samples - taps) // STEP
    bins = bin_count // n
    span = 2 * bins
    all_pulses = n * pulses
    blocks = bin_count // BLOCK
    group = max(4, blocks // 4)
    assert BLOCK % bins == 0 and channels * 2 * span == LANES
    assert BLOCK + bins <= LANES // 2 and samples % (8 * LANES) == 0
    assert blocks % group == 0 and blocks > group and all_pulses % LANES == 0
    depth = taps + 2 * LANES
    samples_out, _, _, az_taps = recon_filters.shape
    step = az_taps // 2
    assert az_taps + step <= LANES
    block = step if whole_image else LANES
    if whole_image:
        turned_rows = all_pulses - step + LANES
        out_shape = (samples_out, 2, bins, all_pulses)
        tt_shape = (samples_out * 2 * step, channels * 2 * LANES)
    else:
        turned_rows = all_pulses
        out_shape = (channels, 2, bins, all_pulses)
        tt_shape = (16, LANES)
    operands = [
        pltpu.with_memory_space_constraint(array, pltpu.HBM)
        for array in (echoes, replica, recon_filters, span_offset, span_width, aperture_edges)
    ]
    vmem = pl.BlockSpec(memory_space=pltpu.VMEM)
    return pl.pallas_call(
        functools.partial(kernel, n, whole_image),
        out_shape=jax.ShapeDtypeStruct(out_shape, jnp.bfloat16),
        in_specs=[pl.BlockSpec(memory_space=pltpu.HBM)] * 6,
        out_specs=vmem,
        scratch_shapes=[
            pltpu.VMEM(replica.shape, jnp.bfloat16),
            pltpu.VMEM(recon_filters.shape, jnp.bfloat16),
            pltpu.SMEM(span_offset.shape, jnp.int32),
            pltpu.SMEM(span_width.shape, jnp.int32),
            pltpu.SMEM(aperture_edges.shape, jnp.int32),
            pltpu.VMEM((2 * channels * pulses, samples + LANES), jnp.bfloat16),
            pltpu.VMEM((LANES, depth), jnp.bfloat16),
            pltpu.VMEM(tt_shape, jnp.bfloat16),
            pltpu.VMEM((2 * channels * bins, LANES), jnp.bfloat16),
            pltpu.VMEM((all_pulses // block * bins, LANES), jnp.float32),
            pltpu.VMEM((channels, group * 2 * pulses, LANES), jnp.float32),
            pltpu.VMEM((n, pulses, LANES), jnp.bfloat16),
            pltpu.VMEM((n, pulses, LANES), jnp.bfloat16),
            pltpu.VMEM((turned_rows, LANES), jnp.float32),
            pltpu.SemaphoreType.DMA((13,)),
            pltpu.SemaphoreType.DMA,
            pltpu.SemaphoreType.DMA,
        ],
        compiler_params=pltpu.CompilerParams(
            collective_id=0, has_side_effects=True, vmem_limit_bytes=32 * 1024 * 1024
        ),
    )(*operands)


def with_neighbours(cells, axis, dim, width):
    count = lax.axis_size(axis)
    head = lax.slice_in_dim(cells, 0, width, axis=dim)
    tail = lax.slice_in_dim(cells, cells.shape[dim] - width, cells.shape[dim], axis=dim)
    up = [(i, i + 1) for i in range(count - 1)]
    down = [(i + 1, i) for i in range(count - 1)]
    return jnp.concatenate(
        [lax.ppermute(tail, axis, up), cells, lax.ppermute(head, axis, down)], axis=dim
    )


def azimuth(padded, filters):
    channels, _, bin_count, padded_len = padded.shape
    subbands = filters.shape[0]
    tap_count = filters.shape[3]
    pulses = padded_len - tap_count
    span_len = tap_count + 4
    step_count = span_len // 4
    quartets = padded.reshape(channels, 2, bin_count, padded_len // 4, 4)
    window = jnp.stack(
        [quartets[:, :, :, first : first + pulses // 4, :] for first in range(step_count)], 4
    )
    window = window.transpose(2, 3, 0, 1, 4, 5).reshape(
        bin_count * (pulses // 4), channels * 2 * span_len
    )
    offset = jnp.arange(span_len)[:, None] - jnp.arange(4)[None, :]
    inside = (offset >= 0) & (offset < tap_count)
    picked = jnp.where(inside, jnp.take(filters, jnp.clip(offset, 0, tap_count - 1), axis=3), 0)
    real, imag = picked[:, :, 0], picked[:, :, 1]
    matrix = jnp.stack([jnp.stack([real, imag], 3), jnp.stack([-imag, real], 3)], 2)
    matrix = matrix.transpose(1, 2, 3, 0, 4, 5).reshape(channels * 2 * span_len, subbands * 8)
    result = jnp.dot(window, matrix, preferred_element_type=jnp.float32)
    result = result.reshape(bin_count, pulses // 4, subbands, 2, 4).transpose(2, 3, 0, 1, 4)
    return result.reshape(subbands, 2, bin_count, pulses)


def body(echoes, replica, recon_filters, span_offset, span_width, aperture_edges):
    operands = (echoes, replica, recon_filters, span_offset, span_width, aperture_edges)
    if lax.axis_size("chan") == 1 and echoes.shape[0] == recon_filters.shape[1]:
        return run_kernel(*operands, whole_image=True)
    corrected = run_kernel(*operands, whole_image=False)
    corrected = lax.all_to_all(corrected, "chan", split_axis=3, concat_axis=0, tiled=True)
    padded = with_neighbours(corrected, "chan", 3, recon_filters.shape[3] // 2)
    return azimuth(padded, recon_filters).astype(jnp.bfloat16)


def solution(mesh):
    return jax.shard_map(
        body,
        mesh=mesh,
        in_specs=(
            P("chan", "pulse", None, None),
            P(),
            P(),
            P("pulse"),
            P("pulse"),
            P(None, "pulse"),
        ),
        out_specs=P(None, None, "pulse", "chan"),
        check_vma=False,
    )
```

```python
import functools

import jax
import jax.numpy as jnp
from jax import lax
from jax.experimental import pallas as pl
from jax.experimental.pallas import tpu as pltpu
from jax.sharding import PartitionSpec as P

LANES = 128
STEP = 4
BLOCK = LANES // STEP
NT = (((1,), (1,)), ((), ()))


def dot_nt(a, b):
    return lax.dot_general(a, b, NT, preferred_element_type=jnp.float32)


def range_rows(replica_ref, bmat_ref, rows, depth):
    taps = replica_ref.shape[1]
    half = bmat_ref.shape[0] // 2
    filled = -(-rows // 16) * 16
    replica = replica_ref[...].astype(jnp.float32)
    for part in range(2):
        row = jnp.concatenate([replica[part : part + 1], jnp.zeros((1, depth - taps), jnp.float32)], axis=1)
        shifted = pltpu.roll(jnp.broadcast_to(row, (rows, depth)), 0, 1, stride=STEP, stride_axis=0)
        shifted = jnp.concatenate([shifted, jnp.zeros((filled - rows, depth), jnp.float32)], axis=0)
        bmat_ref[part * half : part * half + filled, :] = shifted.astype(jnp.bfloat16)


def azimuth_rows(filters_ref, tt_ref, step):
    samples, channels, _, taps = filters_ref.shape
    for s in range(samples):
        for c in range(channels):
            taps_row = filters_ref[s, c].astype(jnp.float32)
            taps_row = jnp.concatenate([taps_row, jnp.zeros((2, LANES - taps), jnp.float32)], axis=1)
            real, imag = [
                pltpu.roll(
                    jnp.broadcast_to(taps_row[part : part + 1], (step, LANES)), 0, 1, stride=1, stride_axis=0
                ).astype(jnp.bfloat16)
                for part in range(2)
            ]
            top, left = s * 2 * step, c * 2 * LANES
            tt_ref[top : top + step, left : left + LANES] = real
            tt_ref[top + step : top + 2 * step, left : left + LANES] = imag
            tt_ref[top : top + step, left + LANES : left + 2 * LANES] = -imag
            tt_ref[top + step : top + 2 * step, left + LANES : left + 2 * LANES] = real


def over(first, last):
    def run(step):
        if last <= 32:
            for k in range(first, last):
                step(k)
        else:
            pl.loop(first, last)(step)

    return run


def column(values, count):
    ids = lax.broadcasted_iota(jnp.int32, (count, LANES), 0)
    total = jnp.zeros((count, LANES), jnp.int32)
    for r in range(count):
        total = jnp.where(ids == r, values(r), total)
    return total


def kernel(
    n, whole_image,
    echoes_in, replica_in, filters_in, offset_in, width_in, edges_in,
    out_ref,
    replica_ref, filters_ref, offset_ref, width_ref, edges_ref,
    lines, bmat, tt, product, send, recv, turned,
    in_sem, send_sem, recv_sem,
):
    me = lax.axis_index("pulse")
    channels, pulses, _, samples = echoes_in.shape
    taps = replica_ref.shape[1]
    depth = bmat.shape[1]
    bin_count = (samples - taps) // STEP
    bins = bin_count // n
    span = 2 * bins
    windows = BLOCK // bins
    pairs = channels * pulses

    echo_rows = echoes_in.reshape(2 * pairs, samples)
    share = samples // 8
    shares = [pl.ds(i * share, share) for i in range(8)]
    echoes_fetches = [
        pltpu.make_async_copy(echo_rows.at[:, at], lines.at[:, at], in_sem.at[5 + i])
        for i, at in enumerate(shares)
    ]
    replica_fetch, *small_fetches = [
        pltpu.make_async_copy(source, held, in_sem.at[i])
        for i, (source, held) in enumerate(
            [
                (replica_in, replica_ref),
                (filters_in, filters_ref),
                (offset_in, offset_ref),
                (width_in, width_ref),
                (edges_in, edges_ref),
            ]
        )
    ]
    for fetch in [replica_fetch, *echoes_fetches, *small_fetches]:
        fetch.start()

    barrier = pltpu.get_barrier_semaphore()

    @over(1, n)
    def _(k):
        pl.semaphore_signal(
            barrier, inc=1, device_id={"pulse": jnp.where(me + k < n, me + k, me + k - n)}, device_id_type=pl.DeviceIdType.MESH
        )

    lines[:, samples:] = jnp.zeros((2 * pairs, lines.shape[1] - samples), lines.dtype)
    half = LANES // 2
    for part in range(2):
        bmat[(part + 1) * half - 16 : (part + 1) * half, :] = jnp.zeros((16, depth), bmat.dtype)
    replica_fetch.wait()
    range_rows(replica_ref, bmat, BLOCK + bins, depth)
    for fetch in echoes_fetches:
        fetch.wait()

    most = product.shape[1] // (2 * pulses)
    blocks = bin_count // BLOCK
    starts = [0, *range(1, blocks, most)]
    rows = 2 * pulses
    for turn, (start, stop) in enumerate(zip(starts, [*starts[1:], blocks])):
        group = stop - start
        targets = group * windows
        lane = lax.broadcasted_iota(jnp.int32, (group * pulses, LANES), 1)
        rows_in = jnp.concatenate(
            [
                lines[:, LANES * (start + a) : LANES * (start + a) + depth]
                for a in range(group)
            ],
            axis=0,
        )
        result = dot_nt(rows_in, bmat[...])
        for a in range(group):
            for c in range(channels):
                at = (a * channels + c) * rows
                product[c, a * rows : (a + 1) * rows, :] = result[at : at + rows]
        by_channel = []
        for c in range(channels):
            from_real = product[c, pl.ds(0, group * pulses, stride=2), :]
            from_imag = pltpu.roll(product[c, pl.ds(1, group * pulses, stride=2), :], half, 1)
            by_channel.append(jnp.where(lane < half, from_real - from_imag, from_real + from_imag))
        for w in range(windows):
            message = None
            for c in range(channels):
                shift = (span * c - bins * w) % LANES
                moved = pltpu.roll(by_channel[c], shift, 1) if shift else by_channel[c]
                message = moved if c == 0 else jnp.where(lane % half >= span * c, moved, message)
            for a in range(group):
                slot = (start + a) * windows + w
                send[slot] = message[a * pulses : (a + 1) * pulses].astype(send.dtype)

        if turn == 0:
            pl.semaphore_wait(barrier, n - 1)

        ahead = 2 if turn == 0 else 0
        others = targets - ahead

        def send_to(to):
            @pl.when(to != me)
            def _():
                pltpu.make_async_remote_copy(
                    src_ref=send.at[to], dst_ref=recv.at[me], send_sem=send_sem, recv_sem=recv_sem,
                    device_id={"pulse": to}, device_id_type=pl.DeviceIdType.MESH,
                ).start()

        for to in range(ahead):
            send_to(to)
        begin = lax.rem(me, others)

        @over(0, others)
        def _(k):
            place = begin + k
            send_to(start * windows + ahead + jnp.where(place < others, place, place - others))

    recv[me] = send[me]

    for fetch in small_fetches:
        fetch.wait()
    all_pulses = n * pulses
    row_id = lax.broadcasted_iota(jnp.int32, (bins, LANES), 0)
    lane_id = lax.broadcasted_iota(jnp.int32, (bins, LANES), 1)
    first_bin = row_id + column(lambda r: offset_ref[r], bins)
    width = column(lambda r: width_ref[r], bins)
    low_edge = column(lambda r: edges_ref[0, r], bins)
    high_edge = all_pulses - column(lambda r: edges_ref[1, r], bins)
    place = lane_id % span
    chosen = (place >= first_bin) & (place < first_bin + width) & (place + me * bins < bin_count)
    select = jnp.concatenate(
        [
            jnp.where(chosen & (lane_id // span == g % 2 * channels + g // 2), 1.0, 0.0)
            for g in range(2 * channels)
        ],
        axis=0,
    ).astype(jnp.bfloat16)
    scale = 1.0 / width.astype(jnp.float32)

    samples_out, _, _, az_taps = filters_ref.shape
    margin = az_taps // 2 if whole_image else 0
    step = tt.shape[0] // (2 * samples_out) if whole_image else LANES
    weights = {}
    for start in range(0, all_pulses, step):
        pulse = lane_id + (start - margin)
        weights[start] = jnp.where((pulse >= low_edge) & (pulse < high_edge), scale, 0.0)
    if whole_image:
        after = turned.shape[0] - margin - all_pulses
        turned[0:margin, :] = jnp.zeros((margin, LANES), jnp.float32)
        turned[margin + all_pulses :, :] = jnp.zeros((after, LANES), jnp.float32)
        azimuth_rows(filters_ref, tt, step)

    pltpu.make_async_copy(send.at[pl.ds(0, n - 1)], recv.at[pl.ds(0, n - 1)], recv_sem).wait()

    for i in range(n):
        turned[margin + i * pulses : margin + (i + 1) * pulses, :] = recv[i].astype(jnp.float32)

    def corrected(start):
        taken = dot_nt(select, turned[start : start + LANES, :].astype(jnp.bfloat16))
        return [taken[g * bins : (g + 1) * bins] * weights[start] for g in range(2 * channels)]

    if whole_image:
        rows_in = jnp.concatenate(
            [jnp.concatenate(corrected(start), axis=1) for start in range(0, all_pulses, step)], axis=0
        ).astype(jnp.bfloat16)
        image = dot_nt(rows_in, tt[...])
        share = LANES // step
        for o in range(2 * samples_out):
            tile, at = o // share, o % share
            for b in range(all_pulses // LANES):
                joined = None
                for i in range(share):
                    top = (b * share + i) * bins
                    part = image[top : top + bins, tile * LANES : (tile + 1) * LANES]
                    shift = (i - at) * step % LANES
                    part = pltpu.roll(part, shift, 1) if shift else part
                    joined = part if i == 0 else jnp.where(lane_id >= i * step, part, joined)
                out_ref[o // 2, o % 2, :, b * LANES : (b + 1) * LANES] = joined.astype(out_ref.dtype)
    else:
        for b in range(all_pulses // LANES):
            for g, part in enumerate(corrected(b * LANES)):
                out_ref[g // 2, g % 2, :, b * LANES : (b + 1) * LANES] = part.astype(out_ref.dtype)

    pltpu.make_async_copy(send.at[pl.ds(0, n - 1)], recv.at[pl.ds(0, n - 1)], send_sem).wait()


def run_kernel(echoes, replica, recon_filters, span_offset, span_width, aperture_edges, whole_image):
    n = lax.axis_size("pulse")
    channels, pulses, _, samples = echoes.shape
    taps = replica.shape[1]
    bin_count = (samples - taps) // STEP
    bins = bin_count // n
    span = 2 * bins
    all_pulses = n * pulses
    blocks = bin_count // BLOCK
    most = min(blocks - 1, 7)
    assert BLOCK % bins == 0 and channels * 2 * span == LANES
    assert BLOCK + bins <= LANES // 2 and samples % (8 * LANES) == 0
    assert blocks > 1 and all_pulses % LANES == 0
    depth = taps + 2 * LANES
    samples_out, _, _, az_taps = recon_filters.shape
    step = az_taps // 2
    assert az_taps + step <= LANES
    if whole_image:
        turned_rows = all_pulses - step + LANES
        out_shape = (samples_out, 2, bins, all_pulses)
        tt_shape = (samples_out * 2 * step, channels * 2 * LANES)
    else:
        turned_rows = all_pulses
        out_shape = (channels, 2, bins, all_pulses)
        tt_shape = (16, LANES)
    operands = [
        pltpu.with_memory_space_constraint(array, pltpu.HBM)
        for array in (echoes, replica, recon_filters, span_offset, span_width, aperture_edges)
    ]
    vmem = pl.BlockSpec(memory_space=pltpu.VMEM)
    return pl.pallas_call(
        functools.partial(kernel, n, whole_image),
        out_shape=jax.ShapeDtypeStruct(out_shape, jnp.bfloat16),
        in_specs=[pl.BlockSpec(memory_space=pltpu.HBM)] * 6,
        out_specs=vmem,
        scratch_shapes=[
            pltpu.VMEM(replica.shape, jnp.bfloat16),
            pltpu.VMEM(recon_filters.shape, jnp.bfloat16),
            pltpu.SMEM(span_offset.shape, jnp.int32),
            pltpu.SMEM(span_width.shape, jnp.int32),
            pltpu.SMEM(aperture_edges.shape, jnp.int32),
            pltpu.VMEM((2 * channels * pulses, samples + LANES), jnp.bfloat16),
            pltpu.VMEM((LANES, depth), jnp.bfloat16),
            pltpu.VMEM(tt_shape, jnp.bfloat16),
            pltpu.VMEM((channels, most * 2 * pulses, LANES), jnp.float32),
            pltpu.VMEM((n, pulses, LANES), jnp.bfloat16),
            pltpu.VMEM((n, pulses, LANES), jnp.bfloat16),
            pltpu.VMEM((turned_rows, LANES), jnp.float32),
            pltpu.SemaphoreType.DMA((13,)),
            pltpu.SemaphoreType.DMA,
            pltpu.SemaphoreType.DMA,
        ],
        compiler_params=pltpu.CompilerParams(
            collective_id=0, has_side_effects=True, vmem_limit_bytes=32 * 1024 * 1024
        ),
    )(*operands)


def with_neighbours(cells, axis, dim, width):
    count = lax.axis_size(axis)
    head = lax.slice_in_dim(cells, 0, width, axis=dim)
    tail = lax.slice_in_dim(cells, cells.shape[dim] - width, cells.shape[dim], axis=dim)
    up = [(i, i + 1) for i in range(count - 1)]
    down = [(i + 1, i) for i in range(count - 1)]
    return jnp.concatenate(
        [lax.ppermute(tail, axis, up), cells, lax.ppermute(head, axis, down)], axis=dim
    )


def azimuth(padded, filters):
    channels, _, bin_count, padded_len = padded.shape
    subbands = filters.shape[0]
    tap_count = filters.shape[3]
    pulses = padded_len - tap_count
    span_len = tap_count + 4
    step_count = span_len // 4
    quartets = padded.reshape(channels, 2, bin_count, padded_len // 4, 4)
    window = jnp.stack(
        [quartets[:, :, :, first : first + pulses // 4, :] for first in range(step_count)], 4
    )
    window = window.transpose(2, 3, 0, 1, 4, 5).reshape(
        bin_count * (pulses // 4), channels * 2 * span_len
    )
    offset = jnp.arange(span_len)[:, None] - jnp.arange(4)[None, :]
    inside = (offset >= 0) & (offset < tap_count)
    picked = jnp.where(inside, jnp.take(filters, jnp.clip(offset, 0, tap_count - 1), axis=3), 0)
    real, imag = picked[:, :, 0], picked[:, :, 1]
    matrix = jnp.stack([jnp.stack([real, imag], 3), jnp.stack([-imag, real], 3)], 2)
    matrix = matrix.transpose(1, 2, 3, 0, 4, 5).reshape(channels * 2 * span_len, subbands * 8)
    result = jnp.dot(window, matrix, preferred_element_type=jnp.float32)
    result = result.reshape(bin_count, pulses // 4, subbands, 2, 4).transpose(2, 3, 0, 1, 4)
    return result.reshape(subbands, 2, bin_count, pulses)


def body(echoes, replica, recon_filters, span_offset, span_width, aperture_edges):
    operands = (echoes, replica, recon_filters, span_offset, span_width, aperture_edges)
    if lax.axis_size("chan") == 1 and echoes.shape[0] == recon_filters.shape[1]:
        return run_kernel(*operands, whole_image=True)
    corrected = run_kernel(*operands, whole_image=False)
    corrected = lax.all_to_all(corrected, "chan", split_axis=3, concat_axis=0, tiled=True)
    padded = with_neighbours(corrected, "chan", 3, recon_filters.shape[3] // 2)
    return azimuth(padded, recon_filters).astype(jnp.bfloat16)


def solution(mesh):
    return jax.shard_map(
        body,
        mesh=mesh,
        in_specs=(
            P("chan", "pulse", None, None),
            P(),
            P(),
            P("pulse"),
            P("pulse"),
            P(None, "pulse"),
        ),
        out_specs=P(None, None, "pulse", "chan"),
        check_vma=False,
    )
```

```python
import functools

import jax
import jax.numpy as jnp
from jax import lax
from jax.experimental import pallas as pl
from jax.experimental.pallas import tpu as pltpu
from jax.sharding import PartitionSpec as P

LANES = 128
STEP = 4
BLOCK = LANES // STEP
NT = (((1,), (1,)), ((), ()))


def dot_nt(a, b):
    return lax.dot_general(a, b, NT, preferred_element_type=jnp.float32)


def range_rows(replica_ref, bmat_ref, rows, depth):
    taps = replica_ref.shape[1]
    half = bmat_ref.shape[0] // 2
    filled = -(-rows // 16) * 16
    replica = replica_ref[...].astype(jnp.float32)
    for part in range(2):
        row = jnp.concatenate([replica[part : part + 1], jnp.zeros((1, depth - taps), jnp.float32)], axis=1)
        shifted = pltpu.roll(jnp.broadcast_to(row, (rows, depth)), 0, 1, stride=STEP, stride_axis=0)
        shifted = jnp.concatenate([shifted, jnp.zeros((filled - rows, depth), jnp.float32)], axis=0)
        bmat_ref[part * half : part * half + filled, :] = shifted.astype(jnp.bfloat16)


def azimuth_rows(filters_ref, tt_ref, step):
    samples, channels, _, taps = filters_ref.shape
    for s in range(samples):
        for c in range(channels):
            taps_row = filters_ref[s, c].astype(jnp.float32)
            taps_row = jnp.concatenate([taps_row, jnp.zeros((2, LANES - taps), jnp.float32)], axis=1)
            real, imag = [
                pltpu.roll(
                    jnp.broadcast_to(taps_row[part : part + 1], (step, LANES)), 0, 1, stride=1, stride_axis=0
                ).astype(jnp.bfloat16)
                for part in range(2)
            ]
            top, left = s * 2 * step, c * 2 * LANES
            tt_ref[top : top + step, left : left + LANES] = real
            tt_ref[top + step : top + 2 * step, left : left + LANES] = imag
            tt_ref[top : top + step, left + LANES : left + 2 * LANES] = -imag
            tt_ref[top + step : top + 2 * step, left + LANES : left + 2 * LANES] = real


def over(first, last):
    def run(step):
        if last <= 2:
            for k in range(first, last):
                step(k)
        else:
            pl.loop(first, last)(step)

    return run


def column(values, count):
    ids = lax.broadcasted_iota(jnp.int32, (count, LANES), 0)
    total = jnp.zeros((count, LANES), jnp.int32)
    for r in range(count):
        total = jnp.where(ids == r, values(r), total)
    return total


def kernel(
    n, whole_image,
    echoes_in, replica_in, filters_in, offset_in, width_in, edges_in,
    out_ref,
    replica_ref, filters_ref, offset_ref, width_ref, edges_ref,
    lines, bmat, tt, product, send, recv, turned,
    in_sem, send_sem, recv_sem,
):
    me = lax.axis_index("pulse")
    channels, pulses, _, samples = echoes_in.shape
    taps = replica_ref.shape[1]
    depth = bmat.shape[1]
    bin_count = (samples - taps) // STEP
    bins = bin_count // n
    span = 2 * bins
    windows = BLOCK // bins
    pairs = channels * pulses

    echo_rows = echoes_in.reshape(2 * pairs, samples)
    share = samples // 8
    shares = [pl.ds(i * share, share) for i in range(8)]
    echoes_fetches = [
        pltpu.make_async_copy(echo_rows.at[:, at], lines.at[:, at], in_sem.at[5 + i])
        for i, at in enumerate(shares)
    ]
    replica_fetch, *small_fetches = [
        pltpu.make_async_copy(source, held, in_sem.at[i])
        for i, (source, held) in enumerate(
            [
                (replica_in, replica_ref),
                (filters_in, filters_ref),
                (offset_in, offset_ref),
                (width_in, width_ref),
                (edges_in, edges_ref),
            ]
        )
    ]
    for fetch in [replica_fetch, *echoes_fetches, *small_fetches]:
        fetch.start()

    barrier = pltpu.get_barrier_semaphore()

    @over(1, n)
    def _(k):
        pl.semaphore_signal(
            barrier, inc=1, device_id={"pulse": jnp.where(me + k < n, me + k, me + k - n)}, device_id_type=pl.DeviceIdType.MESH
        )

    lines[:, samples:] = jnp.zeros((2 * pairs, lines.shape[1] - samples), lines.dtype)
    half = LANES // 2
    for part in range(2):
        bmat[(part + 1) * half - 16 : (part + 1) * half, :] = jnp.zeros((16, depth), bmat.dtype)
    replica_fetch.wait()
    range_rows(replica_ref, bmat, BLOCK + bins, depth)
    for fetch in echoes_fetches:
        fetch.wait()

    group = product.shape[1] // (2 * pulses)
    groups = bin_count // BLOCK // group
    targets = group * windows
    rows = 2 * pulses
    lane = lax.broadcasted_iota(jnp.int32, (group * pulses, LANES), 1)
    for turn in range(groups):
        rows_in = jnp.concatenate(
            [
                lines[:, LANES * (turn * group + a) : LANES * (turn * group + a) + depth]
                for a in range(group)
            ],
            axis=0,
        )
        result = dot_nt(rows_in, bmat[...])
        for a in range(group):
            for c in range(channels):
                at = (a * channels + c) * rows
                product[c, a * rows : (a + 1) * rows, :] = result[at : at + rows]
        by_channel = []
        for c in range(channels):
            from_real = product[c, pl.ds(0, group * pulses, stride=2), :]
            from_imag = pltpu.roll(product[c, pl.ds(1, group * pulses, stride=2), :], half, 1)
            by_channel.append(jnp.where(lane < half, from_real - from_imag, from_real + from_imag))
        for w in range(windows):
            message = None
            for c in range(channels):
                shift = (span * c - bins * w) % LANES
                moved = pltpu.roll(by_channel[c], shift, 1) if shift else by_channel[c]
                message = moved if c == 0 else jnp.where(lane % half >= span * c, moved, message)
            for a in range(group):
                slot = (turn * group + a) * windows + w
                send[slot] = message[a * pulses : (a + 1) * pulses].astype(send.dtype)

        if turn == 0:
            pl.semaphore_wait(barrier, n - 1)

        ahead = 2 if turn == 0 else 0
        others = targets - ahead

        def send_to(to):
            @pl.when(to != me)
            def _():
                pltpu.make_async_remote_copy(
                    src_ref=send.at[to], dst_ref=recv.at[me], send_sem=send_sem, recv_sem=recv_sem,
                    device_id={"pulse": to}, device_id_type=pl.DeviceIdType.MESH,
                ).start()

        for to in range(ahead):
            send_to(to)
        begin = lax.rem(me, others)

        @over(0, others)
        def _(k):
            place = begin + k
            send_to(turn * targets + ahead + jnp.where(place < others, place, place - others))

    recv[me] = send[me]

    for fetch in small_fetches:
        fetch.wait()
    all_pulses = n * pulses
    row_id = lax.broadcasted_iota(jnp.int32, (bins, LANES), 0)
    lane_id = lax.broadcasted_iota(jnp.int32, (bins, LANES), 1)
    first_bin = row_id + column(lambda r: offset_ref[r], bins)
    width = column(lambda r: width_ref[r], bins)
    low_edge = column(lambda r: edges_ref[0, r], bins)
    high_edge = all_pulses - column(lambda r: edges_ref[1, r], bins)
    place = lane_id % span
    chosen = (place >= first_bin) & (place < first_bin + width) & (place + me * bins < bin_count)
    select = jnp.concatenate(
        [
            jnp.where(chosen & (lane_id // span == g % 2 * channels + g // 2), 1.0, 0.0)
            for g in range(2 * channels)
        ],
        axis=0,
    ).astype(jnp.bfloat16)
    scale = 1.0 / width.astype(jnp.float32)

    samples_out, _, _, az_taps = filters_ref.shape
    margin = az_taps // 2 if whole_image else 0
    step = tt.shape[0] // (2 * samples_out) if whole_image else LANES
    weights = {}
    for start in range(0, all_pulses, step):
        pulse = lane_id + (start - margin)
        weights[start] = jnp.where((pulse >= low_edge) & (pulse < high_edge), scale, 0.0)
    if whole_image:
        after = turned.shape[0] - margin - all_pulses
        turned[0:margin, :] = jnp.zeros((margin, LANES), jnp.float32)
        turned[margin + all_pulses :, :] = jnp.zeros((after, LANES), jnp.float32)
        azimuth_rows(filters_ref, tt, step)

    pltpu.make_async_copy(send.at[pl.ds(0, n - 1)], recv.at[pl.ds(0, n - 1)], recv_sem).wait()

    for i in range(n):
        turned[margin + i * pulses : margin + (i + 1) * pulses, :] = recv[i].astype(jnp.float32)

    def corrected(start):
        taken = dot_nt(select, turned[start : start + LANES, :].astype(jnp.bfloat16))
        return [taken[g * bins : (g + 1) * bins] * weights[start] for g in range(2 * channels)]

    if whole_image:
        rows_in = jnp.concatenate(
            [jnp.concatenate(corrected(start), axis=1) for start in range(0, all_pulses, step)], axis=0
        ).astype(jnp.bfloat16)
        image = dot_nt(rows_in, tt[...])
        share = LANES // step
        for o in range(2 * samples_out):
            tile, at = o // share, o % share
            for b in range(all_pulses // LANES):
                joined = None
                for i in range(share):
                    top = (b * share + i) * bins
                    part = image[top : top + bins, tile * LANES : (tile + 1) * LANES]
                    shift = (i - at) * step % LANES
                    part = pltpu.roll(part, shift, 1) if shift else part
                    joined = part if i == 0 else jnp.where(lane_id >= i * step, part, joined)
                out_ref[o // 2, o % 2, :, b * LANES : (b + 1) * LANES] = joined.astype(out_ref.dtype)
    else:
        for b in range(all_pulses // LANES):
            for g, part in enumerate(corrected(b * LANES)):
                out_ref[g // 2, g % 2, :, b * LANES : (b + 1) * LANES] = part.astype(out_ref.dtype)

    pltpu.make_async_copy(send.at[pl.ds(0, n - 1)], recv.at[pl.ds(0, n - 1)], send_sem).wait()


def run_kernel(echoes, replica, recon_filters, span_offset, span_width, aperture_edges, whole_image):
    n = lax.axis_size("pulse")
    channels, pulses, _, samples = echoes.shape
    taps = replica.shape[1]
    bin_count = (samples - taps) // STEP
    bins = bin_count // n
    span = 2 * bins
    all_pulses = n * pulses
    blocks = bin_count // BLOCK
    group = max(4, blocks // 4)
    assert BLOCK % bins == 0 and channels * 2 * span == LANES
    assert BLOCK + bins <= LANES // 2 and samples % (8 * LANES) == 0
    assert blocks % group == 0 and all_pulses % LANES == 0
    depth = taps + 2 * LANES
    samples_out, _, _, az_taps = recon_filters.shape
    step = az_taps // 2
    assert az_taps + step <= LANES
    if whole_image:
        turned_rows = all_pulses - step + LANES
        out_shape = (samples_out, 2, bins, all_pulses)
        tt_shape = (samples_out * 2 * step, channels * 2 * LANES)
    else:
        turned_rows = all_pulses
        out_shape = (channels, 2, bins, all_pulses)
        tt_shape = (16, LANES)
    operands = [
        pltpu.with_memory_space_constraint(array, pltpu.HBM)
        for array in (echoes, replica, recon_filters, span_offset, span_width, aperture_edges)
    ]
    vmem = pl.BlockSpec(memory_space=pltpu.VMEM)
    return pl.pallas_call(
        functools.partial(kernel, n, whole_image),
        out_shape=jax.ShapeDtypeStruct(out_shape, jnp.bfloat16),
        in_specs=[pl.BlockSpec(memory_space=pltpu.HBM)] * 6,
        out_specs=vmem,
        scratch_shapes=[
            pltpu.VMEM(replica.shape, jnp.bfloat16),
            pltpu.VMEM(recon_filters.shape, jnp.bfloat16),
            pltpu.SMEM(span_offset.shape, jnp.int32),
            pltpu.SMEM(span_width.shape, jnp.int32),
            pltpu.SMEM(aperture_edges.shape, jnp.int32),
            pltpu.VMEM((2 * channels * pulses, samples + LANES), jnp.bfloat16),
            pltpu.VMEM((LANES, depth), jnp.bfloat16),
            pltpu.VMEM(tt_shape, jnp.bfloat16),
            pltpu.VMEM((channels, group * 2 * pulses, LANES), jnp.float32),
            pltpu.VMEM((n, pulses, LANES), jnp.bfloat16),
            pltpu.VMEM((n, pulses, LANES), jnp.bfloat16),
            pltpu.VMEM((turned_rows, LANES), jnp.float32),
            pltpu.SemaphoreType.DMA((13,)),
            pltpu.SemaphoreType.DMA,
            pltpu.SemaphoreType.DMA,
        ],
        compiler_params=pltpu.CompilerParams(
            collective_id=0, has_side_effects=True, vmem_limit_bytes=32 * 1024 * 1024
        ),
    )(*operands)


def with_neighbours(cells, axis, dim, width):
    count = lax.axis_size(axis)
    head = lax.slice_in_dim(cells, 0, width, axis=dim)
    tail = lax.slice_in_dim(cells, cells.shape[dim] - width, cells.shape[dim], axis=dim)
    up = [(i, i + 1) for i in range(count - 1)]
    down = [(i + 1, i) for i in range(count - 1)]
    return jnp.concatenate(
        [lax.ppermute(tail, axis, up), cells, lax.ppermute(head, axis, down)], axis=dim
    )


def azimuth(padded, filters):
    channels, _, bin_count, padded_len = padded.shape
    subbands = filters.shape[0]
    tap_count = filters.shape[3]
    pulses = padded_len - tap_count
    span_len = tap_count + 4
    step_count = span_len // 4
    quartets = padded.reshape(channels, 2, bin_count, padded_len // 4, 4)
    window = jnp.stack(
        [quartets[:, :, :, first : first + pulses // 4, :] for first in range(step_count)], 4
    )
    window = window.transpose(2, 3, 0, 1, 4, 5).reshape(
        bin_count * (pulses // 4), channels * 2 * span_len
    )
    offset = jnp.arange(span_len)[:, None] - jnp.arange(4)[None, :]
    inside = (offset >= 0) & (offset < tap_count)
    picked = jnp.where(inside, jnp.take(filters, jnp.clip(offset, 0, tap_count - 1), axis=3), 0)
    real, imag = picked[:, :, 0], picked[:, :, 1]
    matrix = jnp.stack([jnp.stack([real, imag], 3), jnp.stack([-imag, real], 3)], 2)
    matrix = matrix.transpose(1, 2, 3, 0, 4, 5).reshape(channels * 2 * span_len, subbands * 8)
    result = jnp.dot(window, matrix, preferred_element_type=jnp.float32)
    result = result.reshape(bin_count, pulses // 4, subbands, 2, 4).transpose(2, 3, 0, 1, 4)
    return result.reshape(subbands, 2, bin_count, pulses)


def body(echoes, replica, recon_filters, span_offset, span_width, aperture_edges):
    operands = (echoes, replica, recon_filters, span_offset, span_width, aperture_edges)
    if lax.axis_size("chan") == 1 and echoes.shape[0] == recon_filters.shape[1]:
        return run_kernel(*operands, whole_image=True)
    corrected = run_kernel(*operands, whole_image=False)
    corrected = lax.all_to_all(corrected, "chan", split_axis=3, concat_axis=0, tiled=True)
    padded = with_neighbours(corrected, "chan", 3, recon_filters.shape[3] // 2)
    return azimuth(padded, recon_filters).astype(jnp.bfloat16)


def solution(mesh):
    return jax.shard_map(
        body,
        mesh=mesh,
        in_specs=(
            P("chan", "pulse", None, None),
            P(),
            P(),
            P("pulse"),
            P("pulse"),
            P(None, "pulse"),
        ),
        out_specs=P(None, None, "pulse", "chan"),
        check_vma=False,
    )
```

```python
import functools

import jax
import jax.numpy as jnp
from jax import lax
from jax.experimental import pallas as pl
from jax.experimental.pallas import tpu as pltpu
from jax.sharding import PartitionSpec as P

LANES = 128
STEP = 4
BLOCK = LANES // STEP
NT = (((1,), (1,)), ((), ()))


def dot_nt(a, b):
    return lax.dot_general(a, b, NT, preferred_element_type=jnp.float32)


def range_rows(replica_ref, bmat_ref, rows, depth):
    taps = replica_ref.shape[1]
    half = bmat_ref.shape[0] // 2
    filled = -(-rows // 16) * 16
    replica = replica_ref[...].astype(jnp.float32)
    for part in range(2):
        row = jnp.concatenate([replica[part : part + 1], jnp.zeros((1, depth - taps), jnp.float32)], axis=1)
        shifted = pltpu.roll(jnp.broadcast_to(row, (rows, depth)), 0, 1, stride=STEP, stride_axis=0)
        shifted = jnp.concatenate([shifted, jnp.zeros((filled - rows, depth), jnp.float32)], axis=0)
        bmat_ref[part * half : part * half + filled, :] = shifted.astype(jnp.bfloat16)


def azimuth_rows(filters_ref, tt_ref, step):
    samples, channels, _, taps = filters_ref.shape
    for s in range(samples):
        for c in range(channels):
            taps_row = filters_ref[s, c].astype(jnp.float32)
            taps_row = jnp.concatenate([taps_row, jnp.zeros((2, LANES - taps), jnp.float32)], axis=1)
            real, imag = [
                pltpu.roll(
                    jnp.broadcast_to(taps_row[part : part + 1], (step, LANES)), 0, 1, stride=1, stride_axis=0
                ).astype(jnp.bfloat16)
                for part in range(2)
            ]
            top, left = s * 2 * step, c * 2 * LANES
            tt_ref[top : top + step, left : left + LANES] = real
            tt_ref[top + step : top + 2 * step, left : left + LANES] = imag
            tt_ref[top : top + step, left + LANES : left + 2 * LANES] = -imag
            tt_ref[top + step : top + 2 * step, left + LANES : left + 2 * LANES] = real


def over(first, last):
    def run(step):
        if last <= 32:
            for k in range(first, last):
                step(k)
        else:
            pl.loop(first, last)(step)

    return run


def column(values, count):
    ids = lax.broadcasted_iota(jnp.int32, (count, LANES), 0)
    total = jnp.zeros((count, LANES), jnp.int32)
    for r in range(count):
        total = jnp.where(ids == r, values(r), total)
    return total


def kernel(
    n, whole_image,
    echoes_in, replica_in, filters_in, offset_in, width_in, edges_in,
    out_ref,
    replica_ref, filters_ref, offset_ref, width_ref, edges_ref,
    lines, bmat, tt, product, send, recv, turned,
    in_sem, send_sem, recv_sem,
):
    me = lax.axis_index("pulse")
    channels, pulses, _, samples = echoes_in.shape
    taps = replica_ref.shape[1]
    depth = bmat.shape[1]
    bin_count = (samples - taps) // STEP
    bins = bin_count // n
    span = 2 * bins
    windows = BLOCK // bins
    pairs = channels * pulses

    echo_rows = echoes_in.reshape(2 * pairs, samples)
    share = samples // 8
    shares = [pl.ds(i * share, share) for i in range(8)]
    echoes_fetches = [
        pltpu.make_async_copy(echo_rows.at[:, at], lines.at[:, at], in_sem.at[5 + i])
        for i, at in enumerate(shares)
    ]
    replica_fetch, *small_fetches = [
        pltpu.make_async_copy(source, held, in_sem.at[i])
        for i, (source, held) in enumerate(
            [
                (replica_in, replica_ref),
                (filters_in, filters_ref),
                (offset_in, offset_ref),
                (width_in, width_ref),
                (edges_in, edges_ref),
            ]
        )
    ]
    for fetch in [replica_fetch, *echoes_fetches, *small_fetches]:
        fetch.start()

    barrier = pltpu.get_barrier_semaphore()

    lines[:, samples:] = jnp.zeros((2 * pairs, lines.shape[1] - samples), lines.dtype)
    half = LANES // 2
    for part in range(2):
        bmat[(part + 1) * half - 16 : (part + 1) * half, :] = jnp.zeros((16, depth), bmat.dtype)
    replica_fetch.wait()
    range_rows(replica_ref, bmat, BLOCK + bins, depth)
    @over(1, n)
    def _(k):
        pl.semaphore_signal(
            barrier, inc=1, device_id={"pulse": jnp.where(me + k < n, me + k, me + k - n)}, device_id_type=pl.DeviceIdType.MESH
        )

    for fetch in echoes_fetches:
        fetch.wait()

    group = product.shape[1] // (2 * pulses)
    groups = bin_count // BLOCK // group
    targets = group * windows
    rows = 2 * pulses
    lane = lax.broadcasted_iota(jnp.int32, (group * pulses, LANES), 1)
    for turn in range(groups):
        rows_in = jnp.concatenate(
            [
                lines[:, LANES * (turn * group + a) : LANES * (turn * group + a) + depth]
                for a in range(group)
            ],
            axis=0,
        )
        result = dot_nt(rows_in, bmat[...])
        for a in range(group):
            for c in range(channels):
                at = (a * channels + c) * rows
                product[c, a * rows : (a + 1) * rows, :] = result[at : at + rows]
        by_channel = []
        for c in range(channels):
            from_real = product[c, pl.ds(0, group * pulses, stride=2), :]
            from_imag = pltpu.roll(product[c, pl.ds(1, group * pulses, stride=2), :], half, 1)
            by_channel.append(jnp.where(lane < half, from_real - from_imag, from_real + from_imag))
        for w in range(windows):
            message = None
            for c in range(channels):
                shift = (span * c - bins * w) % LANES
                moved = pltpu.roll(by_channel[c], shift, 1) if shift else by_channel[c]
                message = moved if c == 0 else jnp.where(lane % half >= span * c, moved, message)
            for a in range(group):
                slot = (turn * group + a) * windows + w
                send[slot] = message[a * pulses : (a + 1) * pulses].astype(send.dtype)

        if turn == 0:
            pl.semaphore_wait(barrier, n - 1)

        ahead = 2 if turn == 0 else 0
        others = targets - ahead

        def send_to(to):
            @pl.when(to != me)
            def _():
                pltpu.make_async_remote_copy(
                    src_ref=send.at[to], dst_ref=recv.at[me], send_sem=send_sem, recv_sem=recv_sem,
                    device_id={"pulse": to}, device_id_type=pl.DeviceIdType.MESH,
                ).start()

        for to in range(ahead):
            send_to(to)
        begin = lax.rem(me, others)

        @over(0, others)
        def _(k):
            place = begin + k
            send_to(turn * targets + ahead + jnp.where(place < others, place, place - others))

    recv[me] = send[me]

    for fetch in small_fetches:
        fetch.wait()
    all_pulses = n * pulses
    row_id = lax.broadcasted_iota(jnp.int32, (bins, LANES), 0)
    lane_id = lax.broadcasted_iota(jnp.int32, (bins, LANES), 1)
    first_bin = row_id + column(lambda r: offset_ref[r], bins)
    width = column(lambda r: width_ref[r], bins)
    low_edge = column(lambda r: edges_ref[0, r], bins)
    high_edge = all_pulses - column(lambda r: edges_ref[1, r], bins)
    place = lane_id % span
    chosen = (place >= first_bin) & (place < first_bin + width) & (place + me * bins < bin_count)
    select = jnp.concatenate(
        [
            jnp.where(chosen & (lane_id // span == g % 2 * channels + g // 2), 1.0, 0.0)
            for g in range(2 * channels)
        ],
        axis=0,
    ).astype(jnp.bfloat16)
    scale = 1.0 / width.astype(jnp.float32)

    samples_out, _, _, az_taps = filters_ref.shape
    margin = az_taps // 2 if whole_image else 0
    step = tt.shape[0] // (2 * samples_out) if whole_image else LANES
    weights = {}
    for start in range(0, all_pulses, step):
        pulse = lane_id + (start - margin)
        weights[start] = jnp.where((pulse >= low_edge) & (pulse < high_edge), scale, 0.0)
    if whole_image:
        after = turned.shape[0] - margin - all_pulses
        turned[0:margin, :] = jnp.zeros((margin, LANES), jnp.float32)
        turned[margin + all_pulses :, :] = jnp.zeros((after, LANES), jnp.float32)
        azimuth_rows(filters_ref, tt, step)

    pltpu.make_async_copy(send.at[pl.ds(0, n - 1)], recv.at[pl.ds(0, n - 1)], recv_sem).wait()

    for i in range(n):
        turned[margin + i * pulses : margin + (i + 1) * pulses, :] = recv[i].astype(jnp.float32)

    def corrected(start):
        taken = dot_nt(select, turned[start : start + LANES, :].astype(jnp.bfloat16))
        return [taken[g * bins : (g + 1) * bins] * weights[start] for g in range(2 * channels)]

    if whole_image:
        rows_in = jnp.concatenate(
            [jnp.concatenate(corrected(start), axis=1) for start in range(0, all_pulses, step)], axis=0
        ).astype(jnp.bfloat16)
        image = dot_nt(rows_in, tt[...])
        share = LANES // step
        for o in range(2 * samples_out):
            tile, at = o // share, o % share
            for b in range(all_pulses // LANES):
                joined = None
                for i in range(share):
                    top = (b * share + i) * bins
                    part = image[top : top + bins, tile * LANES : (tile + 1) * LANES]
                    shift = (i - at) * step % LANES
                    part = pltpu.roll(part, shift, 1) if shift else part
                    joined = part if i == 0 else jnp.where(lane_id >= i * step, part, joined)
                out_ref[o // 2, o % 2, :, b * LANES : (b + 1) * LANES] = joined.astype(out_ref.dtype)
    else:
        for b in range(all_pulses // LANES):
            for g, part in enumerate(corrected(b * LANES)):
                out_ref[g // 2, g % 2, :, b * LANES : (b + 1) * LANES] = part.astype(out_ref.dtype)

    pltpu.make_async_copy(send.at[pl.ds(0, n - 1)], recv.at[pl.ds(0, n - 1)], send_sem).wait()


def run_kernel(echoes, replica, recon_filters, span_offset, span_width, aperture_edges, whole_image):
    n = lax.axis_size("pulse")
    channels, pulses, _, samples = echoes.shape
    taps = replica.shape[1]
    bin_count = (samples - taps) // STEP
    bins = bin_count // n
    span = 2 * bins
    all_pulses = n * pulses
    blocks = bin_count // BLOCK
    group = max(4, blocks // 4)
    assert BLOCK % bins == 0 and channels * 2 * span == LANES
    assert BLOCK + bins <= LANES // 2 and samples % (8 * LANES) == 0
    assert blocks % group == 0 and all_pulses % LANES == 0
    depth = taps + 2 * LANES
    samples_out, _, _, az_taps = recon_filters.shape
    step = az_taps // 2
    assert az_taps + step <= LANES
    if whole_image:
        turned_rows = all_pulses - step + LANES
        out_shape = (samples_out, 2, bins, all_pulses)
        tt_shape = (samples_out * 2 * step, channels * 2 * LANES)
    else:
        turned_rows = all_pulses
        out_shape = (channels, 2, bins, all_pulses)
        tt_shape = (16, LANES)
    operands = [
        pltpu.with_memory_space_constraint(array, pltpu.HBM)
        for array in (echoes, replica, recon_filters, span_offset, span_width, aperture_edges)
    ]
    vmem = pl.BlockSpec(memory_space=pltpu.VMEM)
    return pl.pallas_call(
        functools.partial(kernel, n, whole_image),
        out_shape=jax.ShapeDtypeStruct(out_shape, jnp.bfloat16),
        in_specs=[pl.BlockSpec(memory_space=pltpu.HBM)] * 6,
        out_specs=vmem,
        scratch_shapes=[
            pltpu.VMEM(replica.shape, jnp.bfloat16),
            pltpu.VMEM(recon_filters.shape, jnp.bfloat16),
            pltpu.SMEM(span_offset.shape, jnp.int32),
            pltpu.SMEM(span_width.shape, jnp.int32),
            pltpu.SMEM(aperture_edges.shape, jnp.int32),
            pltpu.VMEM((2 * channels * pulses, samples + LANES), jnp.bfloat16),
            pltpu.VMEM((LANES, depth), jnp.bfloat16),
            pltpu.VMEM(tt_shape, jnp.bfloat16),
            pltpu.VMEM((channels, group * 2 * pulses, LANES), jnp.float32),
            pltpu.VMEM((n, pulses, LANES), jnp.bfloat16),
            pltpu.VMEM((n, pulses, LANES), jnp.bfloat16),
            pltpu.VMEM((turned_rows, LANES), jnp.float32),
            pltpu.SemaphoreType.DMA((13,)),
            pltpu.SemaphoreType.DMA,
            pltpu.SemaphoreType.DMA,
        ],
        compiler_params=pltpu.CompilerParams(
            collective_id=0, has_side_effects=True, vmem_limit_bytes=32 * 1024 * 1024
        ),
    )(*operands)


def with_neighbours(cells, axis, dim, width):
    count = lax.axis_size(axis)
    head = lax.slice_in_dim(cells, 0, width, axis=dim)
    tail = lax.slice_in_dim(cells, cells.shape[dim] - width, cells.shape[dim], axis=dim)
    up = [(i, i + 1) for i in range(count - 1)]
    down = [(i + 1, i) for i in range(count - 1)]
    return jnp.concatenate(
        [lax.ppermute(tail, axis, up), cells, lax.ppermute(head, axis, down)], axis=dim
    )


def azimuth(padded, filters):
    channels, _, bin_count, padded_len = padded.shape
    subbands = filters.shape[0]
    tap_count = filters.shape[3]
    pulses = padded_len - tap_count
    span_len = tap_count + 4
    step_count = span_len // 4
    quartets = padded.reshape(channels, 2, bin_count, padded_len // 4, 4)
    window = jnp.stack(
        [quartets[:, :, :, first : first + pulses // 4, :] for first in range(step_count)], 4
    )
    window = window.transpose(2, 3, 0, 1, 4, 5).reshape(
        bin_count * (pulses // 4), channels * 2 * span_len
    )
    offset = jnp.arange(span_len)[:, None] - jnp.arange(4)[None, :]
    inside = (offset >= 0) & (offset < tap_count)
    picked = jnp.where(inside, jnp.take(filters, jnp.clip(offset, 0, tap_count - 1), axis=3), 0)
    real, imag = picked[:, :, 0], picked[:, :, 1]
    matrix = jnp.stack([jnp.stack([real, imag], 3), jnp.stack([-imag, real], 3)], 2)
    matrix = matrix.transpose(1, 2, 3, 0, 4, 5).reshape(channels * 2 * span_len, subbands * 8)
    result = jnp.dot(window, matrix, preferred_element_type=jnp.float32)
    result = result.reshape(bin_count, pulses // 4, subbands, 2, 4).transpose(2, 3, 0, 1, 4)
    return result.reshape(subbands, 2, bin_count, pulses)


def body(echoes, replica, recon_filters, span_offset, span_width, aperture_edges):
    operands = (echoes, replica, recon_filters, span_offset, span_width, aperture_edges)
    if lax.axis_size("chan") == 1 and echoes.shape[0] == recon_filters.shape[1]:
        return run_kernel(*operands, whole_image=True)
    corrected = run_kernel(*operands, whole_image=False)
    corrected = lax.all_to_all(corrected, "chan", split_axis=3, concat_axis=0, tiled=True)
    padded = with_neighbours(corrected, "chan", 3, recon_filters.shape[3] // 2)
    return azimuth(padded, recon_filters).astype(jnp.bfloat16)


def solution(mesh):
    return jax.shard_map(
        body,
        mesh=mesh,
        in_specs=(
            P("chan", "pulse", None, None),
            P(),
            P(),
            P("pulse"),
            P("pulse"),
            P(None, "pulse"),
        ),
        out_specs=P(None, None, "pulse", "chan"),
        check_vma=False,
    )
```
